32 devices in a mesh: head: 2 (over x), blk: 16 (over z, y, core).
Axes of the slice: x: 2, y: 2, z: 4, core: 2. Of those that a mesh axis runs over, the one named last changes fastest.
Arguments:
- queries: bfloat16 [2048, 4096], P(('head', 'blk')), may hold values from -6 to 6
- keys: bfloat16 [2048, 1024], P(('head', 'blk')), may hold values from -6 to 6
- values: bfloat16 [2048, 1024], P(('head', 'blk')), may hold values from -6 to 6
- grad_out: bfloat16 [2048, 4096], P(('head', 'blk')), may hold values from -6 to 6
- order: int32 [32], replicated, may hold values from 0 to 31, each once
Outputs:
- grad_queries: bfloat16 [2048, 4096], P(('head', 'blk'))
- grad_keys: bfloat16 [2048, 1024], P(('head', 'blk'))
- grad_values: bfloat16 [2048, 1024], P(('head', 'blk'))
The draws below stay inside these ranges and needn't reach their ends.
Inputs may be any that keep to these rules, and one draw needn't show every extreme that they name: `order`: each value names one slot's pair of half-blocks, each exactly once.
All inputs are finite; a program needn't handle non-finite values.
Results may differ from the reference program's by a relative error of at most 0.024.
Values may be sent and summed in bfloat16 or wider, within the bound.
A program may use at most 64 MiB of HBM per device.

```python
import jax
import jax.numpy as jnp
from jax import lax

TOK_DEV = 64
QH = 32
KVH = 8
HD = 128
REACH = 1
SLOTS = 32
TOKENS = 2048
N_HEAD = 2
N_BLK = 16


def draw_queries(key, part):
    base = jax.random.fold_in(key, 3)
    drawn = jnp.clip(jax.random.normal(base, (TOKENS, QH * HD), jnp.float32), -6.0, 6.0)
    return drawn.astype(jnp.bfloat16)


def draw_keys(key, part):
    base = jax.random.fold_in(key, 5)
    drawn = jnp.clip(jax.random.normal(base, (TOKENS, KVH * HD), jnp.float32), -6.0, 6.0)
    return drawn.astype(jnp.bfloat16)


def steps_of(stream_key, dims, shards, low, largest):
    factor_of, own = 1.0, jax.random.fold_in(stream_key, 6)
    for dim, parts in shards:
        heights = jnp.exp(jax.random.uniform(jax.random.fold_in(own, dim), (parts,), jnp.float32, low / len(shards), largest / len(shards)))
        factor_of = factor_of * jnp.repeat(heights, dims[dim] // parts).reshape([-1 if axis == dim else 1 for axis in range(len(dims))])
    return factor_of


def normal_values(stream_key, extent, scale, most, pieces=(), kind=jnp.bfloat16):
    gain = steps_of(stream_key, extent, pieces, -0.22, 0.18) if pieces else 1.0
    result = jax.random.normal(stream_key, extent, jnp.float32) * scale * gain
    return jnp.minimum(jnp.maximum(result, -most), most).astype(kind)


def setup_inputs(seed: int = 0) -> dict:
    key_list = jax.random.split(jax.random.key(seed), 6)
    queries = draw_queries(jax.random.fold_in(key_list[5], 71), 0)
    keys = draw_keys(jax.random.fold_in(key_list[5], 71), 0)
    values = normal_values(key_list[2], (TOKENS, KVH * HD), 1.0, 6.0, ((0, 32),))
    grad_out = normal_values(key_list[3], (TOKENS, QH * HD), 1.0, 6.0, ((0, 32),))
    order = jax.random.permutation(key_list[4], SLOTS).astype(jnp.int32)
    return dict(queries=queries, keys=keys, values=values, grad_out=grad_out, order=order)


def by_class(values_in, heads):
    shaped = values_in.reshape(N_HEAD, N_BLK, TOK_DEV, heads, HD).transpose(1, 0, 2, 3, 4)
    return shaped.reshape(N_BLK, N_HEAD * TOK_DEV, heads, HD)


def class_positions(order, block_class):
    local_rows = jnp.arange(N_HEAD * TOK_DEV, dtype=jnp.int32)
    slot_index = (local_rows // TOK_DEV) * N_BLK + block_class
    offset_in = local_rows % TOK_DEV
    half_rows = TOK_DEV // 2
    slot_place = order[slot_index]
    early_pos = slot_place * half_rows + offset_in
    late_pos = (2 * SLOTS - 1 - slot_place) * half_rows + offset_in - half_rows
    return jnp.where(offset_in < half_rows, early_pos, late_pos)


def to_storage(stacked, column_count):
    shaped = stacked.reshape(N_BLK, N_HEAD, TOK_DEV, column_count).transpose(1, 0, 2, 3)
    return shaped.reshape(N_HEAD * N_BLK * TOK_DEV, column_count)


def reference(queries, keys, values, grad_out, order):
    score_scale = HD ** -0.5
    row_count = N_HEAD * TOK_DEV
    group_size = QH // KVH
    query_all = by_class(queries, QH)
    key_all = by_class(keys, KVH)
    value_all = by_class(values, KVH)
    grad_all = by_class(grad_out, QH)
    late_rows = (jnp.arange(row_count, dtype=jnp.int32) % TOK_DEV) >= TOK_DEV // 2
    cycle_visible = late_rows[:, None] & jnp.logical_not(late_rows)[None, :]

    def per_class(running, block_class):
        key_acc, value_acc = running
        query_rows = query_all[block_class].astype(jnp.float32).reshape(row_count, KVH, group_size, HD)
        grad_rows = grad_all[block_class].astype(jnp.float32).reshape(row_count, KVH, group_size, HD)
        sources = [(block_class - offset) % N_BLK for offset in range(REACH + 1)]
        key_block = jnp.concatenate([key_all[source] for source in sources], axis=0).astype(jnp.float32)
        value_block = jnp.concatenate([value_all[source] for source in sources], axis=0).astype(jnp.float32)
        query_pos = class_positions(order, block_class)
        own_visible = query_pos[None, :] <= query_pos[:, None]
        visible = jnp.concatenate([own_visible] + [cycle_visible] * REACH, axis=1)
        logits = jnp.einsum("ikgd,jkd->kgij", query_rows, key_block) * score_scale
        row_top = jnp.max(jnp.where(visible, logits, -jnp.inf), axis=-1, keepdims=True)
        row_total = jnp.sum(jnp.where(visible, jnp.exp(logits - row_top), 0.0), axis=-1, keepdims=True)
        log_total = row_top + jnp.log(row_total)
        weights = jnp.where(visible, jnp.exp(logits - log_total), 0.0)
        weights_low = lax.optimization_barrier(weights.astype(jnp.bfloat16)).astype(jnp.float32)
        spread = jnp.einsum("ikgd,jkd->kgij", grad_rows, value_block)
        row_delta = jnp.sum(weights_low * spread, axis=-1, keepdims=True)
        slopes = lax.optimization_barrier((weights * (spread - row_delta)).astype(jnp.bfloat16)).astype(jnp.float32)
        query_grad = (jnp.einsum("kgij,jkd->ikgd", slopes, key_block) * score_scale).astype(jnp.bfloat16)
        key_grad = jnp.einsum("kgij,ikgd->jkd", slopes, query_rows) * score_scale
        value_grad = jnp.einsum("kgij,ikgd->jkd", weights_low, grad_rows)
        for offset in range(REACH + 1):
            source = sources[offset]
            key_acc = key_acc.at[source].add(key_grad[offset * row_count:(offset + 1) * row_count])
            value_acc = value_acc.at[source].add(value_grad[offset * row_count:(offset + 1) * row_count])
        return (key_acc, value_acc), query_grad.reshape(row_count, QH * HD)

    start = (jnp.zeros((N_BLK, row_count, KVH, HD), jnp.float32), jnp.zeros((N_BLK, row_count, KVH, HD), jnp.float32))
    finals, query_grads = lax.scan(per_class, start, jnp.arange(N_BLK, dtype=jnp.int32))
    key_acc, value_acc = finals
    grad_queries = to_storage(query_grads, QH * HD)
    grad_keys = to_storage(key_acc.reshape(N_BLK, row_count, KVH * HD), KVH * HD).astype(jnp.bfloat16)
    grad_values = to_storage(value_acc.reshape(N_BLK, row_count, KVH * HD), KVH * HD).astype(jnp.bfloat16)
    return (grad_queries, grad_keys, grad_values)
```

```python
import functools
import math

import jax
import jax.numpy as jnp
from jax import lax
from jax.experimental import pallas as pl
from jax.experimental.pallas import tpu as pltpu
from jax.sharding import PartitionSpec as P

MESH = pl.DeviceIdType.MESH
HD = 128
CHUNKS = 4
HIDDEN = -1e30


def rows_dot(left, right):
    return lax.dot_general(
        left, right, (((1,), (1,)), ((), ())), preferred_element_type=jnp.float32
    )


def plain_dot(left, right):
    return jnp.dot(left, right, preferred_element_type=jnp.float32)


def cols_dot(left, right):
    return lax.dot_general(
        left, right, (((0,), (0,)), ((), ())), preferred_element_type=jnp.float32
    )


def kernel(
    n, m, slots, chunks,
    order, q_hbm, k_hbm, v_hbm, g_hbm, dq_hbm, dk_hbm, dv_hbm,
    q, g, dq, kv, part, early, own_grad, prev_out, prev_in, part_out, part_in, result,
    bias_early, bias_other,
    load_sem, part_s, part_r, near_s, near_r, far_s, far_r,
    prev_s, prev_r, late_s, late_r, front_s, front_r, dq_sem, out_sem,
):
    head, blk = lax.axis_index("head"), lax.axis_index("blk")
    rows, key_cols = kv.shape[1], kv.shape[2]
    half = rows // 2
    width = key_cols // chunks
    group = q.shape[1] // key_cols
    lanes = group * half
    heads_in = width // HD
    scale = HD ** -0.5
    ahead = (head, lax.rem(blk + 1, m))
    behind = (head, lax.rem(blk + m - 1, m))
    up = [None] + [(lax.rem(head + d, n), blk) for d in range(1, n)]
    down = [None] + [(lax.rem(head + n - d, n), blk) for d in range(1, n)]

    loads = [
        pltpu.make_async_copy(k_hbm, kv.at[0], load_sem.at[0]),
        pltpu.make_async_copy(v_hbm, kv.at[1], load_sem.at[1]),
        pltpu.make_async_copy(q_hbm, q, load_sem.at[2]),
        pltpu.make_async_copy(g_hbm, g, load_sem.at[3]),
    ]
    for load in loads:
        load.start()

    barrier = pltpu.get_barrier_semaphore()
    for other in up[1:] + [ahead, behind]:
        pl.semaphore_signal(barrier, inc=1, device_id=other, device_id_type=MESH)

    mine = order[head * m + blk]
    row = lax.broadcasted_iota(jnp.int32, (half, lanes), 0)
    col = lax.rem(lax.broadcasted_iota(jnp.int32, (half, lanes), 1), half)
    causal = jnp.where(row <= col, 0.0, HIDDEN)
    blank = jnp.zeros((half, lanes), jnp.float32)
    bias_early[pl.ds(0, half), pl.ds(0, lanes)] = causal
    bias_other[pl.ds(0, half), :] = causal
    for d in range(n):
        bias_early[pl.ds(d * half, half), pl.ds(lanes, lanes)] = blank
        bias_other[pl.ds((n + d) * half, half), :] = blank
        if d > 0:
            theirs = order[lax.rem(head + n - d, n) * m + blk]
            first = jnp.where(theirs < mine, 0.0, HIDDEN)
            bias_early[pl.ds(d * half, half), pl.ds(0, lanes)] = blank + first
            bias_other[pl.ds(d * half, half), :] = blank + (HIDDEN - first)

    def span(c):
        return pl.ds(c * width, width)

    def remote(src, dst, send, recv, where):
        return pltpu.make_async_remote_copy(
            src_ref=src, dst_ref=dst, send_sem=send, recv_sem=recv,
            device_id=where, device_id_type=MESH,
        )

    def to_part(d, c):
        return remote(
            kv.at[:, :, span(c)], part.at[d - 1, :, :, span(c)],
            part_s.at[d - 1, c], part_r.at[d - 1, c], up[d],
        )

    def to_near(c):
        return remote(
            kv.at[:, pl.ds(0, half), span(c)], early.at[0, :, :, span(c)],
            near_s.at[c], near_r.at[c], ahead,
        )

    def to_far(d, c):
        return remote(
            part.at[d - 1, :, pl.ds(0, half), span(c)], early.at[d, :, :, span(c)],
            far_s.at[d - 1, c], far_r.at[d - 1, c], ahead,
        )

    def to_prev(c):
        return remote(
            prev_out.at[:, :, :, span(c)], prev_in.at[:, :, :, span(c)],
            prev_s.at[c], prev_r.at[c], behind,
        )

    def to_late(d, c):
        piece = (d - 1, slice(None), pl.ds(half, half), span(c))
        return remote(
            part_out.at[piece], part_in.at[piece],
            late_s.at[d - 1, c], late_r.at[d - 1, c], down[d],
        )

    def to_front(d, c):
        piece = (d - 1, slice(None), pl.ds(0, half), span(c))
        return remote(
            part_out.at[piece], part_in.at[piece],
            front_s.at[d - 1, c], front_r.at[d - 1, c], down[d],
        )

    def dq_copy(c):
        cols = pl.ds(c * width * group, width * group)
        return pltpu.make_async_copy(dq.at[:, cols], dq_hbm.at[:, cols], dq_sem.at[c])

    def out_copy(i, c):
        target = (dk_hbm, dv_hbm)[i]
        return pltpu.make_async_copy(
            result.at[i, :, span(c)], target.at[:, span(c)], out_sem.at[i, c]
        )

    loads[0].wait()
    loads[1].wait()
    pl.semaphore_wait(barrier, n + 1)
    for c in range(chunks):
        for d in range(1, n):
            to_part(d, c).start()
        to_near(c).start()

    def stacked(array, kv_head):
        cols = [pl.ds((kv_head * group + k) * HD, HD) for k in range(group)]
        return jnp.concatenate(
            [array[pl.ds(0, half), col] for col in cols]
            + [array[pl.ds(half, half), col] for col in cols],
            axis=0,
        )

    def one_head(kv_head):
        cols = pl.ds(kv_head * HD, HD)
        lo, hi = pl.ds(0, half), pl.ds(half, half)

        def sources(i):
            first = [kv[i, lo, cols]] + [part[d - 1, i, lo, cols] for d in range(1, n)]
            rest = [kv[i, hi, cols]] + [part[d - 1, i, hi, cols] for d in range(1, n)]
            rest += [early[d, i, :, cols] for d in range(n)]
            return jnp.concatenate(first, axis=0), jnp.concatenate(rest, axis=0)

        key_first, key_rest = sources(0)
        value_first, value_rest = sources(1)
        queries, grads = stacked(q, kv_head), stacked(g, kv_head)
        late_queries, late_grads = queries[lanes:], grads[lanes:]
        factor = scale * math.log2(math.e)
        logits_first = rows_dot(key_first, queries) * factor + bias_early[...]
        logits_rest = rows_dot(key_rest, late_queries) * factor + bias_other[...]
        spread_first = rows_dot(value_first, grads)
        spread_rest = rows_dot(value_rest, late_grads)

        def both(reduce, combine, first, rest):
            whole = reduce(first, axis=0, keepdims=True)
            tail = combine(whole[:, lanes:], reduce(rest, axis=0, keepdims=True))
            return jnp.concatenate([whole[:, :lanes], tail], axis=1)

        top = both(jnp.max, jnp.maximum, logits_first, logits_rest)
        mass_first = jnp.exp2(logits_first - top)
        mass_rest = jnp.exp2(logits_rest - top[:, lanes:])
        inverse = 1.0 / both(jnp.sum, jnp.add, mass_first, mass_rest)
        weights_first = mass_first * inverse
        weights_rest = mass_rest * inverse[:, lanes:]
        delta = both(
            jnp.sum, jnp.add, weights_first * spread_first, weights_rest * spread_rest
        )
        slopes_first = (weights_first * (spread_first - delta)).astype(jnp.bfloat16)
        slopes_rest = (weights_rest * (spread_rest - delta[:, lanes:])).astype(jnp.bfloat16)
        weights_first = weights_first.astype(jnp.bfloat16)
        weights_rest = weights_rest.astype(jnp.bfloat16)

        query_first = cols_dot(slopes_first, key_first)
        query_rest = cols_dot(slopes_rest, key_rest)
        query_grad = (
            jnp.concatenate([query_first[:lanes], query_first[lanes:] + query_rest], axis=0)
            * scale
        ).astype(jnp.bfloat16)
        for k in range(group):
            out = pl.ds((kv_head * group + k) * HD, HD)
            dq[lo, out] = query_grad[k * half : (k + 1) * half]
            dq[hi, out] = query_grad[lanes + k * half : lanes + (k + 1) * half]
        grads_first = (
            plain_dot(slopes_first, queries) * scale,
            plain_dot(weights_first, grads),
        )
        grads_rest = (
            plain_dot(slopes_rest, late_queries) * scale,
            plain_dot(weights_rest, late_grads),
        )
        for i in range(2):
            own_grad[i, lo, cols] = grads_first[i][:half]
            own_grad[i, hi, cols] = grads_rest[i][:half]
            for d in range(1, n):
                at = d * half
                part_out[d - 1, i, lo, cols] = grads_first[i][at : at + half].astype(jnp.bfloat16)
                part_out[d - 1, i, hi, cols] = grads_rest[i][at : at + half].astype(jnp.bfloat16)
            for d in range(n):
                at = (n + d) * half
                prev_out[d, i, :, cols] = grads_rest[i][at : at + half].astype(jnp.bfloat16)

    def stage_arrive(c):
        for d in range(1, n):
            to_part(d, c).wait_recv()
            to_far(d, c).start()

    def stage_compute(c):
        to_near(c).wait_recv()
        for d in range(1, n):
            to_far(d, c).wait_recv()
        if c == 0:
            loads[2].wait()
            loads[3].wait()
        for index in range(heads_in):
            one_head(c * heads_in + index)
        to_prev(c).start()
        for d in range(1, n):
            to_late(d, c).start()
        dq_copy(c).start()

    def stage_front(c):
        to_prev(c).wait_recv()
        for d in range(1, n):
            for i in range(2):
                spot = (d - 1, i, pl.ds(0, half), span(c))
                total = part_out[spot].astype(jnp.float32)
                total = total + prev_in[d, i, :, span(c)].astype(jnp.float32)
                part_out[spot] = total.astype(jnp.bfloat16)
            to_front(d, c).start()

    def stage_finish(c):
        for d in range(1, n):
            to_late(d, c).wait_recv()
            to_front(d, c).wait_recv()
        for i in range(2):
            total = own_grad[i, :, span(c)]
            for d in range(1, n):
                total = total + part_in[d - 1, i, :, span(c)].astype(jnp.float32)
            front = total[:half] + prev_in[0, i, :, span(c)].astype(jnp.float32)
            result[i, pl.ds(0, half), span(c)] = front.astype(jnp.bfloat16)
            result[i, pl.ds(half, half), span(c)] = total[half:].astype(jnp.bfloat16)
            out_copy(i, c).start()

    for t in range(chunks + 2):
        if t < chunks:
            stage_arrive(t)
        if 0 <= t - 1 < chunks:
            stage_compute(t - 1)
        if 0 <= t - 2 < chunks:
            stage_front(t - 2)
    for c in range(chunks):
        stage_finish(c)
    for c in range(chunks):
        to_near(c).wait_send()
        to_prev(c).wait_send()
        for d in range(1, n):
            to_part(d, c).wait_send()
            to_far(d, c).wait_send()
            to_late(d, c).wait_send()
            to_front(d, c).wait_send()
        dq_copy(c).wait()
        out_copy(0, c).wait()
        out_copy(1, c).wait()


def solution(mesh):
    n, m = mesh.shape["head"], mesh.shape["blk"]

    def body(queries, keys, values, grad_out, order):
        rows, query_cols = queries.shape
        key_cols = keys.shape[1]
        half = rows // 2
        chunks = min(CHUNKS, key_cols // HD)
        lanes = half * (query_cols // key_cols)
        low, wide = jnp.bfloat16, jnp.float32
        dma = pltpu.SemaphoreType.DMA
        anywhere = pl.BlockSpec(memory_space=pl.ANY)
        return pl.pallas_call(
            functools.partial(kernel, n, m, order.shape[0], chunks),
            out_shape=(
                jax.ShapeDtypeStruct(queries.shape, low),
                jax.ShapeDtypeStruct(keys.shape, low),
                jax.ShapeDtypeStruct(values.shape, low),
            ),
            in_specs=[pl.BlockSpec(memory_space=pltpu.SMEM)] + [anywhere] * 4,
            out_specs=[anywhere] * 3,
            scratch_shapes=[
                pltpu.VMEM((rows, query_cols), low),
                pltpu.VMEM((rows, query_cols), low),
                pltpu.VMEM((rows, query_cols), low),
                pltpu.VMEM((2, rows, key_cols), low),
                pltpu.VMEM((n - 1, 2, rows, key_cols), low),
                pltpu.VMEM((n, 2, half, key_cols), low),
                pltpu.VMEM((2, rows, key_cols), wide),
                pltpu.VMEM((n, 2, half, key_cols), low),
                pltpu.VMEM((n, 2, half, key_cols), low),
                pltpu.VMEM((n - 1, 2, rows, key_cols), low),
                pltpu.VMEM((n - 1, 2, rows, key_cols), low),
                pltpu.VMEM((2, rows, key_cols), low),
                pltpu.VMEM((n * half, 2 * lanes), wide),
                pltpu.VMEM((2 * n * half, lanes), wide),
                dma((4,)),
                dma((n - 1, chunks)), dma((n - 1, chunks)),
                dma((chunks,)), dma((chunks,)),
                dma((n - 1, chunks)), dma((n - 1, chunks)),
                dma((chunks,)), dma((chunks,)),
                dma((n - 1, chunks)), dma((n - 1, chunks)),
                dma((n - 1, chunks)), dma((n - 1, chunks)),
                dma((chunks,)), dma((2, chunks)),
            ],
            compiler_params=pltpu.CompilerParams(
                collective_id=0, has_side_effects=True, vmem_limit_bytes=40 * 2**20
            ),
        )(order, queries, keys, values, grad_out)

    shard = P(("head", "blk"), None)
    return jax.shard_map(
        body,
        mesh=mesh,
        in_specs=(shard, shard, shard, shard, P()),
        out_specs=(shard, shard, shard),
        check_vma=False,
    )
```

```python
import functools
import math

import jax
import jax.numpy as jnp
from jax import lax
from jax.experimental import pallas as pl
from jax.experimental.pallas import tpu as pltpu
from jax.sharding import PartitionSpec as P

MESH = pl.DeviceIdType.MESH
HD = 128
CHUNKS = 4
HIDDEN = -1e30


def rows_dot(left, right):
    return lax.dot_general(
        left, right, (((1,), (1,)), ((), ())), preferred_element_type=jnp.float32
    )


def plain_dot(left, right):
    return jnp.dot(left, right, preferred_element_type=jnp.float32)


def cols_dot(left, right):
    return lax.dot_general(
        left, right, (((0,), (0,)), ((), ())), preferred_element_type=jnp.float32
    )


def kernel(
    n, m, slots, chunks,
    order_hbm, q_hbm, k_hbm, v_hbm, g_hbm, dq_hbm, dk_hbm, dv_hbm,
    q, g, dq, kv, part, early, own_grad, prev_out, prev_in, part_out, part_in, result,
    bias_early, bias_other, order,
    load_sem, head_s, head_r, tail_s, tail_r, near_s, near_r, far_s, far_r,
    prev_s, prev_r, late_s, late_r, front_s, front_r, dq_sem, out_sem,
):
    head, blk = lax.axis_index("head"), lax.axis_index("blk")
    rows, key_cols = kv.shape[1], kv.shape[2]
    half = rows // 2
    width = key_cols // chunks
    group = q.shape[1] // key_cols
    lanes = group * half
    heads_in = width // HD
    scale = HD ** -0.5
    ahead = (head, lax.rem(blk + 1, m))
    behind = (head, lax.rem(blk + m - 1, m))
    up = [None] + [(lax.rem(head + d, n), blk) for d in range(1, n)]
    down = [None] + [(lax.rem(head + n - d, n), blk) for d in range(1, n)]

    loads = [
        pltpu.make_async_copy(k_hbm, kv.at[0], load_sem.at[0]),
        pltpu.make_async_copy(v_hbm, kv.at[1], load_sem.at[1]),
        pltpu.make_async_copy(q_hbm, q, load_sem.at[2]),
        pltpu.make_async_copy(g_hbm, g, load_sem.at[3]),
        pltpu.make_async_copy(order_hbm, order, load_sem.at[4]),
    ]
    for load in loads:
        load.start()

    barrier = pltpu.get_barrier_semaphore()
    for other in up[1:] + [ahead, behind]:
        pl.semaphore_signal(barrier, inc=1, device_id=other, device_id_type=MESH)

    def span(c):
        return pl.ds(c * width, width)

    def remote(src, dst, send, recv, where):
        return pltpu.make_async_remote_copy(
            src_ref=src, dst_ref=dst, send_sem=send, recv_sem=recv,
            device_id=where, device_id_type=MESH,
        )

    def to_part(d, c, late):
        piece = (slice(None), pl.ds(half if late else 0, half), span(c))
        sends, recvs = (tail_s, tail_r) if late else (head_s, head_r)
        return remote(
            kv.at[piece], part.at[(d - 1,) + piece],
            sends.at[d - 1, c], recvs.at[d - 1, c], up[d],
        )

    def to_near(c):
        return remote(
            kv.at[:, pl.ds(0, half), span(c)], early.at[0, :, :, span(c)],
            near_s.at[c], near_r.at[c], ahead,
        )

    def to_far(d, c):
        return remote(
            part.at[d - 1, :, pl.ds(0, half), span(c)], early.at[d, :, :, span(c)],
            far_s.at[d - 1, c], far_r.at[d - 1, c], ahead,
        )

    def to_prev(c):
        return remote(
            prev_out.at[:, :, :, span(c)], prev_in.at[:, :, :, span(c)],
            prev_s.at[c], prev_r.at[c], behind,
        )

    def to_late(d, c):
        piece = (d - 1, slice(None), pl.ds(half, half), span(c))
        return remote(
            part_out.at[piece], part_in.at[piece],
            late_s.at[d - 1, c], late_r.at[d - 1, c], down[d],
        )

    def to_front(d, c):
        piece = (d - 1, slice(None), pl.ds(0, half), span(c))
        return remote(
            part_out.at[piece], part_in.at[piece],
            front_s.at[d - 1, c], front_r.at[d - 1, c], down[d],
        )

    def dq_copy(c):
        cols = pl.ds(c * width * group, width * group)
        return pltpu.make_async_copy(dq.at[:, cols], dq_hbm.at[:, cols], dq_sem.at[c])

    def out_copy(i, c):
        target = (dk_hbm, dv_hbm)[i]
        return pltpu.make_async_copy(
            result.at[i, :, span(c)], target.at[:, span(c)], out_sem.at[i, c]
        )

    loads[0].wait()
    loads[1].wait()
    pl.semaphore_wait(barrier, n + 1)
    for c in range(chunks):
        for d in range(1, n):
            to_part(d, c, False).start()
        to_near(c).start()

    loads[4].wait()
    mine = order[head * m + blk]
    row = lax.broadcasted_iota(jnp.int32, (half, lanes), 0)
    col = lax.rem(lax.broadcasted_iota(jnp.int32, (half, lanes), 1), half)
    causal = jnp.where(row <= col, 0.0, HIDDEN)
    blank = jnp.zeros((half, lanes), jnp.float32)
    bias_early[pl.ds(0, half), pl.ds(0, lanes)] = causal
    bias_other[pl.ds(0, half), :] = causal
    for d in range(n):
        bias_early[pl.ds(d * half, half), pl.ds(lanes, lanes)] = blank
        bias_other[pl.ds((n + d) * half, half), :] = blank
        if d > 0:
            theirs = order[lax.rem(head + n - d, n) * m + blk]
            first = jnp.where(theirs < mine, 0.0, HIDDEN)
            bias_early[pl.ds(d * half, half), pl.ds(0, lanes)] = blank + first
            bias_other[pl.ds(d * half, half), :] = blank + (HIDDEN - first)

    def stacked(array, kv_head):
        cols = [pl.ds((kv_head * group + k) * HD, HD) for k in range(group)]
        return jnp.concatenate(
            [array[pl.ds(0, half), col] for col in cols]
            + [array[pl.ds(half, half), col] for col in cols],
            axis=0,
        )

    def one_head(kv_head):
        cols = pl.ds(kv_head * HD, HD)
        lo, hi = pl.ds(0, half), pl.ds(half, half)

        def sources(i):
            first = [kv[i, lo, cols]] + [part[d - 1, i, lo, cols] for d in range(1, n)]
            rest = [kv[i, hi, cols]] + [part[d - 1, i, hi, cols] for d in range(1, n)]
            rest += [early[d, i, :, cols] for d in range(n)]
            return jnp.concatenate(first, axis=0), jnp.concatenate(rest, axis=0)

        key_first, key_rest = sources(0)
        value_first, value_rest = sources(1)
        queries, grads = stacked(q, kv_head), stacked(g, kv_head)
        late_queries, late_grads = queries[lanes:], grads[lanes:]
        factor = scale * math.log2(math.e)
        logits_first = rows_dot(key_first, queries) * factor + bias_early[...]
        logits_rest = rows_dot(key_rest, late_queries) * factor + bias_other[...]
        spread_first = rows_dot(value_first, grads)
        spread_rest = rows_dot(value_rest, late_grads)

        def both(reduce, combine, first, rest):
            whole = reduce(first, axis=0, keepdims=True)
            tail = combine(whole[:, lanes:], reduce(rest, axis=0, keepdims=True))
            return jnp.concatenate([whole[:, :lanes], tail], axis=1)

        top = both(jnp.max, jnp.maximum, logits_first, logits_rest)
        mass_first = jnp.exp2(logits_first - top)
        mass_rest = jnp.exp2(logits_rest - top[:, lanes:])
        inverse = 1.0 / both(jnp.sum, jnp.add, mass_first, mass_rest)
        weights_first = mass_first * inverse
        weights_rest = mass_rest * inverse[:, lanes:]
        delta = both(
            jnp.sum, jnp.add, weights_first * spread_first, weights_rest * spread_rest
        )
        slopes_first = (weights_first * (spread_first - delta)).astype(jnp.bfloat16)
        slopes_rest = (weights_rest * (spread_rest - delta[:, lanes:])).astype(jnp.bfloat16)
        weights_first = weights_first.astype(jnp.bfloat16)
        weights_rest = weights_rest.astype(jnp.bfloat16)

        query_first = cols_dot(slopes_first, key_first)
        query_rest = cols_dot(slopes_rest, key_rest)
        query_grad = (
            jnp.concatenate([query_first[:lanes], query_first[lanes:] + query_rest], axis=0)
            * scale
        ).astype(jnp.bfloat16)
        for k in range(group):
            out = pl.ds((kv_head * group + k) * HD, HD)
            dq[lo, out] = query_grad[k * half : (k + 1) * half]
            dq[hi, out] = query_grad[lanes + k * half : lanes + (k + 1) * half]
        grads_first = (
            plain_dot(slopes_first, queries) * scale,
            plain_dot(weights_first, grads),
        )
        grads_rest = (
            plain_dot(slopes_rest, late_queries) * scale,
            plain_dot(weights_rest, late_grads),
        )
        for i in range(2):
            own_grad[i, lo, cols] = grads_first[i][:half]
            own_grad[i, hi, cols] = grads_rest[i][:half]
            for d in range(1, n):
                at = d * half
                part_out[d - 1, i, lo, cols] = grads_first[i][at : at + half].astype(jnp.bfloat16)
                part_out[d - 1, i, hi, cols] = grads_rest[i][at : at + half].astype(jnp.bfloat16)
            for d in range(n):
                at = (n + d) * half
                prev_out[d, i, :, cols] = grads_rest[i][at : at + half].astype(jnp.bfloat16)

    def stage_arrive(c):
        for d in range(1, n):
            to_part(d, c, False).wait_recv()
            to_far(d, c).start()
            to_part(d, c, True).start()

    def stage_compute(c):
        to_near(c).wait_recv()
        for d in range(1, n):
            to_far(d, c).wait_recv()
            to_part(d, c, True).wait_recv()
        if c == 0:
            loads[2].wait()
            loads[3].wait()
        for index in range(heads_in):
            one_head(c * heads_in + index)
        to_prev(c).start()
        for d in range(1, n):
            to_late(d, c).start()
        dq_copy(c).start()

    def stage_front(c):
        to_prev(c).wait_recv()
        for d in range(1, n):
            for i in range(2):
                spot = (d - 1, i, pl.ds(0, half), span(c))
                total = part_out[spot].astype(jnp.float32)
                total = total + prev_in[d, i, :, span(c)].astype(jnp.float32)
                part_out[spot] = total.astype(jnp.bfloat16)
            to_front(d, c).start()

    def stage_finish(c):
        for d in range(1, n):
            to_late(d, c).wait_recv()
            to_front(d, c).wait_recv()
        for i in range(2):
            total = own_grad[i, :, span(c)]
            for d in range(1, n):
                total = total + part_in[d - 1, i, :, span(c)].astype(jnp.float32)
            front = total[:half] + prev_in[0, i, :, span(c)].astype(jnp.float32)
            result[i, pl.ds(0, half), span(c)] = front.astype(jnp.bfloat16)
            result[i, pl.ds(half, half), span(c)] = total[half:].astype(jnp.bfloat16)
            out_copy(i, c).start()

    for stage in (stage_arrive, stage_compute, stage_front):
        for c in range(chunks):
            stage(c)
    for c in range(chunks):
        stage_finish(c)
    for c in range(chunks):
        to_near(c).wait_send()
        to_prev(c).wait_send()
        for d in range(1, n):
            to_part(d, c, False).wait_send()
            to_part(d, c, True).wait_send()
            to_far(d, c).wait_send()
            to_late(d, c).wait_send()
            to_front(d, c).wait_send()
        dq_copy(c).wait()
        out_copy(0, c).wait()
        out_copy(1, c).wait()


def hand_over(a, b, c, a_out, b_out, c_out, sem):
    rows = a.shape[0] // 4
    pairs = [(b, b_out), (c, c_out)]
    for i in range(4):
        pairs.append((a.at[pl.ds(i * rows, rows)], a_out.at[pl.ds(i * rows, rows)]))
    copies = [
        pltpu.make_async_copy(src, dst, sem.at[i]) for i, (src, dst) in enumerate(pairs)
    ]
    for copy in copies:
        copy.start()
    for copy in copies:
        copy.wait()


def solution(mesh):
    n, m = mesh.shape["head"], mesh.shape["blk"]

    def body(queries, keys, values, grad_out, order):
        rows, query_cols = queries.shape
        key_cols = keys.shape[1]
        half = rows // 2
        chunks = min(CHUNKS, key_cols // HD)
        lanes = half * (query_cols // key_cols)
        low, wide = jnp.bfloat16, jnp.float32
        dma = pltpu.SemaphoreType.DMA
        anywhere = pl.BlockSpec(memory_space=pl.ANY)
        grads = pl.pallas_call(
            functools.partial(kernel, n, m, order.shape[0], chunks),
            out_shape=(
                jax.ShapeDtypeStruct(queries.shape, low),
                jax.ShapeDtypeStruct(keys.shape, low),
                jax.ShapeDtypeStruct(values.shape, low),
            ),
            in_specs=[anywhere] * 5,
            out_specs=[anywhere] * 3,
            scratch_shapes=[
                pltpu.VMEM((rows, query_cols), low),
                pltpu.VMEM((rows, query_cols), low),
                pltpu.VMEM((rows, query_cols), low),
                pltpu.VMEM((2, rows, key_cols), low),
                pltpu.VMEM((n - 1, 2, rows, key_cols), low),
                pltpu.VMEM((n, 2, half, key_cols), low),
                pltpu.VMEM((2, rows, key_cols), wide),
                pltpu.VMEM((n, 2, half, key_cols), low),
                pltpu.VMEM((n, 2, half, key_cols), low),
                pltpu.VMEM((n - 1, 2, rows, key_cols), low),
                pltpu.VMEM((n - 1, 2, rows, key_cols), low),
                pltpu.VMEM((2, rows, key_cols), low),
                pltpu.VMEM((n * half, 2 * lanes), wide),
                pltpu.VMEM((2 * n * half, lanes), wide),
                pltpu.SMEM(order.shape, order.dtype),
                dma((5,)),
                dma((n - 1, chunks)), dma((n - 1, chunks)),
                dma((n - 1, chunks)), dma((n - 1, chunks)),
                dma((chunks,)), dma((chunks,)),
                dma((n - 1, chunks)), dma((n - 1, chunks)),
                dma((chunks,)), dma((chunks,)),
                dma((n - 1, chunks)), dma((n - 1, chunks)),
                dma((n - 1, chunks)), dma((n - 1, chunks)),
                dma((chunks,)), dma((2, chunks)),
            ],
            compiler_params=pltpu.CompilerParams(
                collective_id=0, has_side_effects=True, vmem_limit_bytes=64 * 2**20 - 2**16
            ),
        )(order, queries, keys, values, grad_out)
        return pl.pallas_call(
            hand_over,
            out_shape=tuple(jax.ShapeDtypeStruct(x.shape, x.dtype) for x in grads),
            in_specs=[anywhere] * 3,
            out_specs=[anywhere] * 3,
            scratch_shapes=[dma((6,))],
            compiler_params=pltpu.CompilerParams(vmem_limit_bytes=64 * 2**20 - 2**16),
        )(*grads)

    shard = P(("head", "blk"), None)
    return jax.shard_map(
        body,
        mesh=mesh,
        in_specs=(shard, shard, shard, shard, P()),
        out_specs=(shard, shard, shard),
        check_vma=False,
    )
```

```python
import functools
import math

import jax
import jax.numpy as jnp
from jax import lax
from jax.experimental import pallas as pl
from jax.experimental.pallas import tpu as pltpu
from jax.sharding import PartitionSpec as P

MESH = pl.DeviceIdType.MESH
HD = 128
CHUNKS = 4
HIDDEN = -1e30


def rows_dot(left, right):
    return lax.dot_general(
        left, right, (((1,), (1,)), ((), ())), preferred_element_type=jnp.float32
    )


def plain_dot(left, right):
    return jnp.dot(left, right, preferred_element_type=jnp.float32)


def cols_dot(left, right):
    return lax.dot_general(
        left, right, (((0,), (0,)), ((), ())), preferred_element_type=jnp.float32
    )


def kernel(
    n, m, slots, chunks,
    order_hbm, q_hbm, k_hbm, v_hbm, g_hbm, dq_hbm, dk_hbm, dv_hbm,
    q, g, dq, kv, part, early, own_grad, prev_out, prev_in, part_out, part_in, result,
    bias_early, bias_other, order,
    load_sem, head_s, head_r, tail_s, tail_r, near_s, near_r, far_s, far_r,
    prev_s, prev_r, late_s, late_r, front_s, front_r, dq_sem, out_sem,
):
    head, blk = lax.axis_index("head"), lax.axis_index("blk")
    rows, key_cols = kv.shape[1], kv.shape[2]
    half = rows // 2
    width = key_cols // chunks
    group = q.shape[1] // key_cols
    lanes = group * half
    heads_in = width // HD
    scale = HD ** -0.5
    ahead = (head, lax.rem(blk + 1, m))
    behind = (head, lax.rem(blk + m - 1, m))
    up = [None] + [(lax.rem(head + d, n), blk) for d in range(1, n)]
    down = [None] + [(lax.rem(head + n - d, n), blk) for d in range(1, n)]

    loads = [
        pltpu.make_async_copy(k_hbm, kv.at[0], load_sem.at[0]),
        pltpu.make_async_copy(v_hbm, kv.at[1], load_sem.at[1]),
        pltpu.make_async_copy(q_hbm, q, load_sem.at[2]),
        pltpu.make_async_copy(g_hbm, g, load_sem.at[3]),
        pltpu.make_async_copy(order_hbm, order, load_sem.at[4]),
    ]
    for load in loads:
        load.start()

    barrier = pltpu.get_barrier_semaphore()
    for other in up[1:] + [ahead, behind]:
        pl.semaphore_signal(barrier, inc=1, device_id=other, device_id_type=MESH)

    def span(c):
        return pl.ds(c * width, width)

    def remote(src, dst, send, recv, where):
        return pltpu.make_async_remote_copy(
            src_ref=src, dst_ref=dst, send_sem=send, recv_sem=recv,
            device_id=where, device_id_type=MESH,
        )

    def to_part(d, c, late):
        piece = (slice(None), pl.ds(half if late else 0, half), span(c))
        sends, recvs = (tail_s, tail_r) if late else (head_s, head_r)
        return remote(
            kv.at[piece], part.at[(d - 1,) + piece],
            sends.at[d - 1, c], recvs.at[d - 1, c], up[d],
        )

    def to_near(c):
        return remote(
            kv.at[:, pl.ds(0, half), span(c)], early.at[0, :, :, span(c)],
            near_s.at[c], near_r.at[c], ahead,
        )

    def to_far(d, c):
        return remote(
            part.at[d - 1, :, pl.ds(0, half), span(c)], early.at[d, :, :, span(c)],
            far_s.at[d - 1, c], far_r.at[d - 1, c], ahead,
        )

    def to_prev(c):
        return remote(
            prev_out.at[:, :, :, span(c)], prev_in.at[:, :, :, span(c)],
            prev_s.at[c], prev_r.at[c], behind,
        )

    def to_late(d, c):
        piece = (d - 1, slice(None), pl.ds(half, half), span(c))
        return remote(
            part_out.at[piece], part_in.at[piece],
            late_s.at[d - 1, c], late_r.at[d - 1, c], down[d],
        )

    def to_front(d, c):
        piece = (d - 1, slice(None), pl.ds(0, half), span(c))
        return remote(
            part_out.at[piece], part_in.at[piece],
            front_s.at[d - 1, c], front_r.at[d - 1, c], down[d],
        )

    def dq_copy(c):
        cols = pl.ds(c * width * group, width * group)
        return pltpu.make_async_copy(dq.at[:, cols], dq_hbm.at[:, cols], dq_sem.at[c])

    def out_copy(i, c):
        target = (dk_hbm, dv_hbm)[i]
        return pltpu.make_async_copy(
            result.at[i, :, span(c)], target.at[:, span(c)], out_sem.at[i, c]
        )

    loads[0].wait()
    loads[1].wait()
    pl.semaphore_wait(barrier, n + 1)
    for c in range(chunks):
        for d in range(1, n):
            to_part(d, c, False).start()
        to_near(c).start()

    loads[4].wait()
    mine = order[head * m + blk]
    row = lax.broadcasted_iota(jnp.int32, (half, lanes), 0)
    col = lax.rem(lax.broadcasted_iota(jnp.int32, (half, lanes), 1), half)
    causal = jnp.where(row <= col, 0.0, HIDDEN)
    blank = jnp.zeros((half, lanes), jnp.float32)
    bias_early[pl.ds(0, half), pl.ds(0, lanes)] = causal
    bias_other[pl.ds(0, half), :] = causal
    for d in range(n):
        bias_early[pl.ds(d * half, half), pl.ds(lanes, lanes)] = blank
        bias_other[pl.ds((n + d) * half, half), :] = blank
        if d > 0:
            theirs = order[lax.rem(head + n - d, n) * m + blk]
            first = jnp.where(theirs < mine, 0.0, HIDDEN)
            bias_early[pl.ds(d * half, half), pl.ds(0, lanes)] = blank + first
            bias_other[pl.ds(d * half, half), :] = blank + (HIDDEN - first)

    def stacked(array, kv_head):
        cols = [pl.ds((kv_head * group + k) * HD, HD) for k in range(group)]
        return jnp.concatenate(
            [array[pl.ds(0, half), col] for col in cols]
            + [array[pl.ds(half, half), col] for col in cols],
            axis=0,
        )

    def one_head(kv_head):
        cols = pl.ds(kv_head * HD, HD)
        lo, hi = pl.ds(0, half), pl.ds(half, half)

        def sources(i):
            first = [kv[i, lo, cols]] + [part[d - 1, i, lo, cols] for d in range(1, n)]
            rest = [kv[i, hi, cols]] + [part[d - 1, i, hi, cols] for d in range(1, n)]
            rest += [early[d, i, :, cols] for d in range(n)]
            return jnp.concatenate(first, axis=0), jnp.concatenate(rest, axis=0)

        key_first, key_rest = sources(0)
        value_first, value_rest = sources(1)
        queries, grads = stacked(q, kv_head), stacked(g, kv_head)
        late_queries, late_grads = queries[lanes:], grads[lanes:]
        factor = scale * math.log2(math.e)
        logits_first = rows_dot(key_first, queries) * factor + bias_early[...]
        logits_rest = rows_dot(key_rest, late_queries) * factor + bias_other[...]
        spread_first = rows_dot(value_first, grads)
        spread_rest = rows_dot(value_rest, late_grads)

        def both(reduce, combine, first, rest):
            whole = reduce(first, axis=0, keepdims=True)
            tail = combine(whole[:, lanes:], reduce(rest, axis=0, keepdims=True))
            return jnp.concatenate([whole[:, :lanes], tail], axis=1)

        top = both(jnp.max, jnp.maximum, logits_first, logits_rest)
        mass_first = jnp.exp2(logits_first - top)
        mass_rest = jnp.exp2(logits_rest - top[:, lanes:])
        inverse = 1.0 / both(jnp.sum, jnp.add, mass_first, mass_rest)
        weights_first = mass_first * inverse
        weights_rest = mass_rest * inverse[:, lanes:]
        delta = both(
            jnp.sum, jnp.add, weights_first * spread_first, weights_rest * spread_rest
        )
        slopes_first = (weights_first * (spread_first - delta)).astype(jnp.bfloat16)
        slopes_rest = (weights_rest * (spread_rest - delta[:, lanes:])).astype(jnp.bfloat16)
        weights_first = weights_first.astype(jnp.bfloat16)
        weights_rest = weights_rest.astype(jnp.bfloat16)

        query_first = cols_dot(slopes_first, key_first)
        query_rest = cols_dot(slopes_rest, key_rest)
        query_grad = (
            jnp.concatenate([query_first[:lanes], query_first[lanes:] + query_rest], axis=0)
            * scale
        ).astype(jnp.bfloat16)
        for k in range(group):
            out = pl.ds((kv_head * group + k) * HD, HD)
            dq[lo, out] = query_grad[k * half : (k + 1) * half]
            dq[hi, out] = query_grad[lanes + k * half : lanes + (k + 1) * half]
        grads_first = (
            plain_dot(slopes_first, queries) * scale,
            plain_dot(weights_first, grads),
        )
        grads_rest = (
            plain_dot(slopes_rest, late_queries) * scale,
            plain_dot(weights_rest, late_grads),
        )
        for i in range(2):
            own_grad[i, lo, cols] = grads_first[i][:half]
            own_grad[i, hi, cols] = grads_rest[i][:half]
            for d in range(1, n):
                at = d * half
                part_out[d - 1, i, lo, cols] = grads_first[i][at : at + half].astype(jnp.bfloat16)
                part_out[d - 1, i, hi, cols] = grads_rest[i][at : at + half].astype(jnp.bfloat16)
            for d in range(n):
                at = (n + d) * half
                prev_out[d, i, :, cols] = grads_rest[i][at : at + half].astype(jnp.bfloat16)

    def stage_arrive(c):
        for d in range(1, n):
            to_part(d, c, False).wait_recv()
            to_far(d, c).start()
            to_part(d, c, True).start()

    def stage_compute(c):
        to_near(c).wait_recv()
        for d in range(1, n):
            to_far(d, c).wait_recv()
            to_part(d, c, True).wait_recv()
        if c == 0:
            loads[2].wait()
            loads[3].wait()
        for index in range(heads_in):
            one_head(c * heads_in + index)
        to_prev(c).start()
        for d in range(1, n):
            to_late(d, c).start()
        dq_copy(c).start()

    def stage_front(c):
        to_prev(c).wait_recv()
        for d in range(1, n):
            for i in range(2):
                spot = (d - 1, i, pl.ds(0, half), span(c))
                total = part_out[spot].astype(jnp.float32)
                total = total + prev_in[d, i, :, span(c)].astype(jnp.float32)
                part_out[spot] = total.astype(jnp.bfloat16)
            to_front(d, c).start()

    def stage_finish(c):
        for d in range(1, n):
            to_late(d, c).wait_recv()
            to_front(d, c).wait_recv()
        for i in range(2):
            total = own_grad[i, :, span(c)]
            for d in range(1, n):
                total = total + part_in[d - 1, i, :, span(c)].astype(jnp.float32)
            front = total[:half] + prev_in[0, i, :, span(c)].astype(jnp.float32)
            result[i, pl.ds(0, half), span(c)] = front.astype(jnp.bfloat16)
            result[i, pl.ds(half, half), span(c)] = total[half:].astype(jnp.bfloat16)
            out_copy(i, c).start()

    for stage in (stage_arrive, stage_compute, stage_front):
        for c in range(chunks):
            stage(c)
    for c in range(chunks):
        stage_finish(c)
    for c in range(chunks):
        to_near(c).wait_send()
        to_prev(c).wait_send()
        for d in range(1, n):
            to_part(d, c, False).wait_send()
            to_part(d, c, True).wait_send()
            to_far(d, c).wait_send()
            to_late(d, c).wait_send()
            to_front(d, c).wait_send()
        dq_copy(c).wait()
        out_copy(0, c).wait()
        out_copy(1, c).wait()


def hand_over(a, b, c, a_out, b_out, c_out, sem):
    rows = a.shape[0] // 4
    pairs = [(b, b_out), (c, c_out)]
    for i in range(4):
        pairs.append((a.at[pl.ds(i * rows, rows)], a_out.at[pl.ds(i * rows, rows)]))
    copies = [
        pltpu.make_async_copy(src, dst, sem.at[i]) for i, (src, dst) in enumerate(pairs)
    ]
    for copy in copies:
        copy.start()
    for copy in copies:
        copy.wait()


def solution(mesh):
    n, m = mesh.shape["head"], mesh.shape["blk"]

    def body(queries, keys, values, grad_out, order):
        rows, query_cols = queries.shape
        key_cols = keys.shape[1]
        half = rows // 2
        chunks = min(CHUNKS, key_cols // HD)
        lanes = half * (query_cols // key_cols)
        low, wide = jnp.bfloat16, jnp.float32
        dma = pltpu.SemaphoreType.DMA
        anywhere = pl.BlockSpec(memory_space=pl.ANY)
        grads = pl.pallas_call(
            functools.partial(kernel, n, m, order.shape[0], chunks),
            out_shape=(
                jax.ShapeDtypeStruct(queries.shape, low),
                jax.ShapeDtypeStruct(keys.shape, low),
                jax.ShapeDtypeStruct(values.shape, low),
            ),
            in_specs=[anywhere] * 5,
            out_specs=[anywhere] * 3,
            scratch_shapes=[
                pltpu.VMEM((rows, query_cols), low),
                pltpu.VMEM((rows, query_cols), low),
                pltpu.VMEM((rows, query_cols), low),
                pltpu.VMEM((2, rows, key_cols), low),
                pltpu.VMEM((n - 1, 2, rows, key_cols), low),
                pltpu.VMEM((n, 2, half, key_cols), low),
                pltpu.VMEM((2, rows, key_cols), wide),
                pltpu.VMEM((n, 2, half, key_cols), low),
                pltpu.VMEM((n, 2, half, key_cols), low),
                pltpu.VMEM((n - 1, 2, rows, key_cols), low),
                pltpu.VMEM((n - 1, 2, rows, key_cols), low),
                pltpu.VMEM((2, rows, key_cols), low),
                pltpu.VMEM((n * half, 2 * lanes), wide),
                pltpu.VMEM((2 * n * half, lanes), wide),
                pltpu.SMEM(order.shape, order.dtype),
                dma((5,)),
                dma((n - 1, chunks)), dma((n - 1, chunks)),
                dma((n - 1, chunks)), dma((n - 1, chunks)),
                dma((chunks,)), dma((chunks,)),
                dma((n - 1, chunks)), dma((n - 1, chunks)),
                dma((chunks,)), dma((chunks,)),
                dma((n - 1, chunks)), dma((n - 1, chunks)),
                dma((n - 1, chunks)), dma((n - 1, chunks)),
                dma((chunks,)), dma((2, chunks)),
            ],
            compiler_params=pltpu.CompilerParams(
                collective_id=0, has_side_effects=True, vmem_limit_bytes=40 * 2**20
            ),
        )(*(
            pltpu.with_memory_space_constraint(x, pltpu.HBM)
            for x in (order, queries, keys, values, grad_out)
        ))
        return pl.pallas_call(
            hand_over,
            out_shape=tuple(jax.ShapeDtypeStruct(x.shape, x.dtype) for x in grads),
            in_specs=[anywhere] * 3,
            out_specs=[anywhere] * 3,
            scratch_shapes=[dma((6,))],
            compiler_params=pltpu.CompilerParams(vmem_limit_bytes=2**20),
        )(*grads)

    shard = P(("head", "blk"), None)
    return jax.shard_map(
        body,
        mesh=mesh,
        in_specs=(shard, shard, shard, shard, P()),
        out_specs=(shard, shard, shard),
        check_vma=False,
    )
```

```python
import functools
import math

import jax
import jax.numpy as jnp
from jax import lax
from jax.experimental import pallas as pl
from jax.experimental.pallas import tpu as pltpu
from jax.sharding import PartitionSpec as P

MESH = pl.DeviceIdType.MESH
HD = 128
CHUNKS = 4
HIDDEN = -1e30


def rows_dot(left, right):
    return lax.dot_general(
        left, right, (((1,), (1,)), ((), ())), preferred_element_type=jnp.float32
    )


def plain_dot(left, right):
    return jnp.dot(left, right, preferred_element_type=jnp.float32)


def cols_dot(left, right):
    return lax.dot_general(
        left, right, (((0,), (0,)), ((), ())), preferred_element_type=jnp.float32
    )


def kernel(
    n, m, slots, chunks,
    order_hbm, q_hbm, k_hbm, v_hbm, g_hbm, dq_hbm, dk_hbm, dv_hbm,
    q, g, dq, kv, part, early, own_grad, prev_out, prev_in, part_out, part_in, result,
    bias_early, bias_other, order, ready,
    load_sem, head_s, head_r, tail_s, tail_r, near_s, near_r, far_s, far_r,
    prev_s, prev_r, late_s, late_r, front_s, front_r, dq_sem, out_sem,
):
    head, blk = lax.axis_index("head"), lax.axis_index("blk")
    rows, key_cols = kv.shape[1], kv.shape[2]
    half = rows // 2
    width = key_cols // chunks
    group = q.shape[1] // key_cols
    lanes = group * half
    heads_in = width // HD
    scale = HD ** -0.5
    ahead = (head, lax.rem(blk + 1, m))
    behind = (head, lax.rem(blk + m - 1, m))
    up = [None] + [(lax.rem(head + d, n), blk) for d in range(1, n)]
    down = [None] + [(lax.rem(head + n - d, n), blk) for d in range(1, n)]

    loads = [
        pltpu.make_async_copy(k_hbm, kv.at[0], load_sem.at[0]),
        pltpu.make_async_copy(v_hbm, kv.at[1], load_sem.at[1]),
        pltpu.make_async_copy(q_hbm, q, load_sem.at[2]),
        pltpu.make_async_copy(g_hbm, g, load_sem.at[3]),
        pltpu.make_async_copy(order_hbm, order, load_sem.at[4]),
    ]
    for load in loads:
        load.start()

    barrier = pltpu.get_barrier_semaphore()
    for other in up[1:] + [ahead, behind]:
        pl.semaphore_signal(barrier, inc=1, device_id=other, device_id_type=MESH)

    def span(c):
        return pl.ds(c * width, width)

    def remote(src, dst, send, recv, where):
        return pltpu.make_async_remote_copy(
            src_ref=src, dst_ref=dst, send_sem=send, recv_sem=recv,
            device_id=where, device_id_type=MESH,
        )

    def to_part(d, c, late):
        piece = (slice(None), pl.ds(half if late else 0, half), span(c))
        sends, recvs = (tail_s, tail_r) if late else (head_s, head_r)
        return remote(
            kv.at[piece], part.at[(d - 1,) + piece],
            sends.at[d - 1, c], recvs.at[d - 1, c], up[d],
        )

    def to_near(c):
        return remote(
            kv.at[:, pl.ds(0, half), span(c)], early.at[0, :, :, span(c)],
            near_s.at[c], near_r.at[c], ahead,
        )

    def to_far(d, c):
        return remote(
            part.at[d - 1, :, pl.ds(0, half), span(c)], early.at[d, :, :, span(c)],
            far_s.at[d - 1, c], far_r.at[d - 1, c], ahead,
        )

    def to_prev(c):
        return remote(
            prev_out.at[:, :, :, span(c)], prev_in.at[:, :, :, span(c)],
            prev_s.at[c], prev_r.at[c], behind,
        )

    def to_late(d, c):
        piece = (d - 1, slice(None), pl.ds(half, half), span(c))
        return remote(
            part_out.at[piece], part_in.at[piece],
            late_s.at[d - 1, c], late_r.at[d - 1, c], down[d],
        )

    def to_front(d, c):
        piece = (d - 1, slice(None), pl.ds(0, half), span(c))
        return remote(
            part_out.at[piece], part_in.at[piece],
            front_s.at[d - 1, c], front_r.at[d - 1, c], down[d],
        )

    def dq_copy(c):
        cols = pl.ds(c * width * group, width * group)
        return pltpu.make_async_copy(dq.at[:, cols], dq_hbm.at[:, cols], dq_sem.at[c])

    def out_copy(i, c):
        target = (dk_hbm, dv_hbm)[i]
        return pltpu.make_async_copy(
            result.at[i, :, span(c)], target.at[:, span(c)], out_sem.at[i, c]
        )

    loads[0].wait()
    loads[1].wait()
    pl.semaphore_wait(barrier, n + 1)
    for c in range(chunks):
        for d in range(1, n):
            to_part(d, c, False).start()
        to_near(c).start()

    loads[4].wait()
    mine = order[head * m + blk]
    row = lax.broadcasted_iota(jnp.int32, (half, lanes), 0)
    col = lax.rem(lax.broadcasted_iota(jnp.int32, (half, lanes), 1), half)
    causal = jnp.where(row <= col, 0.0, HIDDEN)
    blank = jnp.zeros((half, lanes), jnp.float32)
    bias_early[pl.ds(0, half), pl.ds(0, lanes)] = causal
    bias_other[pl.ds(0, half), :] = causal
    for d in range(n):
        bias_early[pl.ds(d * half, half), pl.ds(lanes, lanes)] = blank
        bias_other[pl.ds((n + d) * half, half), :] = blank
        if d > 0:
            theirs = order[lax.rem(head + n - d, n) * m + blk]
            first = jnp.where(theirs < mine, 0.0, HIDDEN)
            bias_early[pl.ds(d * half, half), pl.ds(0, lanes)] = blank + first
            bias_other[pl.ds(d * half, half), :] = blank + (HIDDEN - first)

    def stacked(array, kv_head):
        cols = [pl.ds((kv_head * group + k) * HD, HD) for k in range(group)]
        return jnp.concatenate(
            [array[pl.ds(0, half), col] for col in cols]
            + [array[pl.ds(half, half), col] for col in cols],
            axis=0,
        )

    lo, hi = pl.ds(0, half), pl.ds(half, half)
    factor = scale * math.log2(math.e)

    def early_keys(i, cols):
        first = [kv[i, lo, cols]] + [part[d - 1, i, lo, cols] for d in range(1, n)]
        return jnp.concatenate(first, axis=0)

    def other_keys(i, cols):
        rest = [kv[i, hi, cols]] + [part[d - 1, i, hi, cols] for d in range(1, n)]
        rest += [early[d, i, :, cols] for d in range(n)]
        return jnp.concatenate(rest, axis=0)

    def first_logits(kv_head):
        cols = pl.ds(kv_head * HD, HD)
        logits = rows_dot(early_keys(0, cols), stacked(q, kv_head))
        ready[kv_head, 0] = logits * factor + bias_early[...]
        ready[kv_head, 1] = rows_dot(early_keys(1, cols), stacked(g, kv_head))

    def one_head(kv_head):
        cols = pl.ds(kv_head * HD, HD)
        key_first, key_rest = early_keys(0, cols), other_keys(0, cols)
        value_rest = other_keys(1, cols)
        queries, grads = stacked(q, kv_head), stacked(g, kv_head)
        late_queries, late_grads = queries[lanes:], grads[lanes:]
        logits_first, spread_first = ready[kv_head, 0], ready[kv_head, 1]
        logits_rest = rows_dot(key_rest, late_queries) * factor + bias_other[...]
        spread_rest = rows_dot(value_rest, late_grads)

        def both(reduce, combine, first, rest):
            whole = reduce(first, axis=0, keepdims=True)
            tail = combine(whole[:, lanes:], reduce(rest, axis=0, keepdims=True))
            return jnp.concatenate([whole[:, :lanes], tail], axis=1)

        top = both(jnp.max, jnp.maximum, logits_first, logits_rest)
        mass_first = jnp.exp2(logits_first - top)
        mass_rest = jnp.exp2(logits_rest - top[:, lanes:])
        inverse = 1.0 / both(jnp.sum, jnp.add, mass_first, mass_rest)
        weights_first = mass_first * inverse
        weights_rest = mass_rest * inverse[:, lanes:]
        delta = both(
            jnp.sum, jnp.add, weights_first * spread_first, weights_rest * spread_rest
        )
        slopes_first = (weights_first * (spread_first - delta)).astype(jnp.bfloat16)
        slopes_rest = (weights_rest * (spread_rest - delta[:, lanes:])).astype(jnp.bfloat16)
        weights_first = weights_first.astype(jnp.bfloat16)
        weights_rest = weights_rest.astype(jnp.bfloat16)

        query_first = cols_dot(slopes_first, key_first)
        query_rest = cols_dot(slopes_rest, key_rest)
        query_grad = (
            jnp.concatenate([query_first[:lanes], query_first[lanes:] + query_rest], axis=0)
            * scale
        ).astype(jnp.bfloat16)
        for k in range(group):
            out = pl.ds((kv_head * group + k) * HD, HD)
            dq[lo, out] = query_grad[k * half : (k + 1) * half]
            dq[hi, out] = query_grad[lanes + k * half : lanes + (k + 1) * half]
        grads_first = (
            plain_dot(slopes_first, queries) * scale,
            plain_dot(weights_first, grads),
        )
        grads_rest = (
            plain_dot(slopes_rest, late_queries) * scale,
            plain_dot(weights_rest, late_grads),
        )
        for i in range(2):
            own_grad[i, lo, cols] = grads_first[i][:half]
            own_grad[i, hi, cols] = grads_rest[i][:half]
            for d in range(1, n):
                at = d * half
                part_out[d - 1, i, lo, cols] = grads_first[i][at : at + half].astype(jnp.bfloat16)
                part_out[d - 1, i, hi, cols] = grads_rest[i][at : at + half].astype(jnp.bfloat16)
            for d in range(n):
                at = (n + d) * half
                prev_out[d, i, :, cols] = grads_rest[i][at : at + half].astype(jnp.bfloat16)

    def stage_arrive(c):
        for d in range(1, n):
            to_part(d, c, False).wait_recv()
            to_far(d, c).start()
            to_part(d, c, True).start()
        if c == 0:
            loads[2].wait()
            loads[3].wait()
        for index in range(heads_in):
            first_logits(c * heads_in + index)

    def stage_compute(c):
        to_near(c).wait_recv()
        for d in range(1, n):
            to_far(d, c).wait_recv()
            to_part(d, c, True).wait_recv()
        for index in range(heads_in):
            one_head(c * heads_in + index)
        to_prev(c).start()
        for d in range(1, n):
            to_late(d, c).start()
        dq_copy(c).start()

    def stage_front(c):
        to_prev(c).wait_recv()
        for d in range(1, n):
            for i in range(2):
                spot = (d - 1, i, pl.ds(0, half), span(c))
                total = part_out[spot].astype(jnp.float32)
                total = total + prev_in[d, i, :, span(c)].astype(jnp.float32)
                part_out[spot] = total.astype(jnp.bfloat16)
            to_front(d, c).start()

    def stage_finish(c):
        for d in range(1, n):
            to_late(d, c).wait_recv()
            to_front(d, c).wait_recv()
        for i in range(2):
            total = own_grad[i, :, span(c)]
            for d in range(1, n):
                total = total + part_in[d - 1, i, :, span(c)].astype(jnp.float32)
            front = total[:half] + prev_in[0, i, :, span(c)].astype(jnp.float32)
            result[i, pl.ds(0, half), span(c)] = front.astype(jnp.bfloat16)
            result[i, pl.ds(half, half), span(c)] = total[half:].astype(jnp.bfloat16)
            out_copy(i, c).start()

    for c in range(chunks):
        stage_arrive(c)
    for t in range(chunks + 2):
        if t < chunks:
            stage_compute(t)
        if t >= 2:
            stage_front(t - 2)
    for c in range(chunks):
        stage_finish(c)
    for c in range(chunks):
        to_near(c).wait_send()
        to_prev(c).wait_send()
        for d in range(1, n):
            to_part(d, c, False).wait_send()
            to_part(d, c, True).wait_send()
            to_far(d, c).wait_send()
            to_late(d, c).wait_send()
            to_front(d, c).wait_send()
        dq_copy(c).wait()
        out_copy(0, c).wait()
        out_copy(1, c).wait()


def hand_over(a, b, c, a_out, b_out, c_out, sem):
    rows = a.shape[0] // 4
    pairs = [(b, b_out), (c, c_out)]
    for i in range(4):
        pairs.append((a.at[pl.ds(i * rows, rows)], a_out.at[pl.ds(i * rows, rows)]))
    copies = [
        pltpu.make_async_copy(src, dst, sem.at[i]) for i, (src, dst) in enumerate(pairs)
    ]
    for copy in copies:
        copy.start()
    for copy in copies:
        copy.wait()


def solution(mesh):
    n, m = mesh.shape["head"], mesh.shape["blk"]

    def body(queries, keys, values, grad_out, order):
        rows, query_cols = queries.shape
        key_cols = keys.shape[1]
        half = rows // 2
        chunks = min(CHUNKS, key_cols // HD)
        lanes = half * (query_cols // key_cols)
        low, wide = jnp.bfloat16, jnp.float32
        dma = pltpu.SemaphoreType.DMA
        anywhere = pl.BlockSpec(memory_space=pl.ANY)
        grads = pl.pallas_call(
            functools.partial(kernel, n, m, order.shape[0], chunks),
            out_shape=(
                jax.ShapeDtypeStruct(queries.shape, low),
                jax.ShapeDtypeStruct(keys.shape, low),
                jax.ShapeDtypeStruct(values.shape, low),
            ),
            in_specs=[anywhere] * 5,
            out_specs=[anywhere] * 3,
            scratch_shapes=[
                pltpu.VMEM((rows, query_cols), low),
                pltpu.VMEM((rows, query_cols), low),
                pltpu.VMEM((rows, query_cols), low),
                pltpu.VMEM((2, rows, key_cols), low),
                pltpu.VMEM((n - 1, 2, rows, key_cols), low),
                pltpu.VMEM((n, 2, half, key_cols), low),
                pltpu.VMEM((2, rows, key_cols), wide),
                pltpu.VMEM((n, 2, half, key_cols), low),
                pltpu.VMEM((n, 2, half, key_cols), low),
                pltpu.VMEM((n - 1, 2, rows, key_cols), low),
                pltpu.VMEM((n - 1, 2, rows, key_cols), low),
                pltpu.VMEM((2, rows, key_cols), low),
                pltpu.VMEM((n * half, 2 * lanes), wide),
                pltpu.VMEM((2 * n * half, lanes), wide),
                pltpu.SMEM(order.shape, order.dtype),
                pltpu.VMEM((key_cols // HD, 2, n * half, 2 * lanes), wide),
                dma((5,)),
                dma((n - 1, chunks)), dma((n - 1, chunks)),
                dma((n - 1, chunks)), dma((n - 1, chunks)),
                dma((chunks,)), dma((chunks,)),
                dma((n - 1, chunks)), dma((n - 1, chunks)),
                dma((chunks,)), dma((chunks,)),
                dma((n - 1, chunks)), dma((n - 1, chunks)),
                dma((n - 1, chunks)), dma((n - 1, chunks)),
                dma((chunks,)), dma((2, chunks)),
            ],
            compiler_params=pltpu.CompilerParams(
                collective_id=0, has_side_effects=True, vmem_limit_bytes=40 * 2**20
            ),
        )(*(
            pltpu.with_memory_space_constraint(x, pltpu.HBM)
            for x in (order, queries, keys, values, grad_out)
        ))
        return pl.pallas_call(
            hand_over,
            out_shape=tuple(jax.ShapeDtypeStruct(x.shape, x.dtype) for x in grads),
            in_specs=[anywhere] * 3,
            out_specs=[anywhere] * 3,
            scratch_shapes=[dma((6,))],
            compiler_params=pltpu.CompilerParams(vmem_limit_bytes=2**20),
        )(*grads)

    shard = P(("head", "blk"), None)
    return jax.shard_map(
        body,
        mesh=mesh,
        in_specs=(shard, shard, shard, shard, P()),
        out_specs=(shard, shard, shard),
        check_vma=False,
    )
```

```python
import functools
import math

import jax
import jax.numpy as jnp
from jax import lax
from jax.experimental import pallas as pl
from jax.experimental.pallas import tpu as pltpu
from jax.sharding import PartitionSpec as P

MESH = pl.DeviceIdType.MESH
HD = 128
CHUNKS = 8
HIDDEN = -1e30


def rows_dot(left, right):
    return lax.dot_general(
        left, right, (((1,), (1,)), ((), ())), preferred_element_type=jnp.float32
    )


def plain_dot(left, right):
    return jnp.dot(left, right, preferred_element_type=jnp.float32)


def cols_dot(left, right):
    return lax.dot_general(
        left, right, (((0,), (0,)), ((), ())), preferred_element_type=jnp.float32
    )


def kernel(
    n, m, slots, chunks,
    order_hbm, q_hbm, k_hbm, v_hbm, g_hbm, dq_hbm, dk_hbm, dv_hbm,
    q, g, dq, kv, part, early, own_grad, prev_out, prev_in, part_out, part_in, result,
    bias_early, bias_other, order, ready,
    load_sem, head_s, head_r, tail_s, tail_r, near_s, near_r, far_s, far_r,
    prev_s, prev_r, late_s, late_r, front_s, front_r, dq_sem, out_sem,
):
    head, blk = lax.axis_index("head"), lax.axis_index("blk")
    rows, key_cols = kv.shape[1], kv.shape[2]
    half = rows // 2
    width = key_cols // chunks
    group = q.shape[1] // key_cols
    lanes = group * half
    heads_in = width // HD
    scale = HD ** -0.5
    ahead = (head, lax.rem(blk + 1, m))
    behind = (head, lax.rem(blk + m - 1, m))
    up = [None] + [(lax.rem(head + d, n), blk) for d in range(1, n)]
    down = [None] + [(lax.rem(head + n - d, n), blk) for d in range(1, n)]

    loads = [
        pltpu.make_async_copy(k_hbm, kv.at[0], load_sem.at[0]),
        pltpu.make_async_copy(v_hbm, kv.at[1], load_sem.at[1]),
        pltpu.make_async_copy(q_hbm, q, load_sem.at[2]),
        pltpu.make_async_copy(g_hbm, g, load_sem.at[3]),
        pltpu.make_async_copy(order_hbm, order, load_sem.at[4]),
    ]
    for load in loads:
        load.start()

    barrier = pltpu.get_barrier_semaphore()
    for other in up[1:] + [ahead, behind]:
        pl.semaphore_signal(barrier, inc=1, device_id=other, device_id_type=MESH)

    def span(c):
        return pl.ds(c * width, width)

    def remote(src, dst, send, recv, where):
        return pltpu.make_async_remote_copy(
            src_ref=src, dst_ref=dst, send_sem=send, recv_sem=recv,
            device_id=where, device_id_type=MESH,
        )

    def to_part(d, c, late):
        piece = (slice(None), pl.ds(half if late else 0, half), span(c))
        sends, recvs = (tail_s, tail_r) if late else (head_s, head_r)
        return remote(
            kv.at[piece], part.at[(d - 1,) + piece],
            sends.at[d - 1, c], recvs.at[d - 1, c], up[d],
        )

    def to_near(c):
        return remote(
            kv.at[:, pl.ds(0, half), span(c)], early.at[0, :, :, span(c)],
            near_s.at[c], near_r.at[c], ahead,
        )

    def to_far(d, c):
        return remote(
            part.at[d - 1, :, pl.ds(0, half), span(c)], early.at[d, :, :, span(c)],
            far_s.at[d - 1, c], far_r.at[d - 1, c], ahead,
        )

    def to_prev(c):
        return remote(
            prev_out.at[:, :, :, span(c)], prev_in.at[:, :, :, span(c)],
            prev_s.at[c], prev_r.at[c], behind,
        )

    def to_late(d, c):
        piece = (d - 1, slice(None), pl.ds(half, half), span(c))
        return remote(
            part_out.at[piece], part_in.at[piece],
            late_s.at[d - 1, c], late_r.at[d - 1, c], down[d],
        )

    def to_front(d, c):
        piece = (d - 1, slice(None), pl.ds(0, half), span(c))
        return remote(
            part_out.at[piece], part_in.at[piece],
            front_s.at[d - 1, c], front_r.at[d - 1, c], down[d],
        )

    def dq_copy(c):
        cols = pl.ds(c * width * group, width * group)
        return pltpu.make_async_copy(dq.at[:, cols], dq_hbm.at[:, cols], dq_sem.at[c])

    def out_copy(i, c):
        target = (dk_hbm, dv_hbm)[i]
        return pltpu.make_async_copy(
            result.at[i, :, span(c)], target.at[:, span(c)], out_sem.at[i, c]
        )

    loads[0].wait()
    loads[1].wait()
    pl.semaphore_wait(barrier, n + 1)
    for c in range(chunks):
        for d in range(1, n):
            to_part(d, c, False).start()
        to_near(c).start()

    loads[4].wait()
    mine = order[head * m + blk]
    row = lax.broadcasted_iota(jnp.int32, (half, lanes), 0)
    col = lax.rem(lax.broadcasted_iota(jnp.int32, (half, lanes), 1), half)
    causal = jnp.where(row <= col, 0.0, HIDDEN)
    blank = jnp.zeros((half, lanes), jnp.float32)
    bias_early[pl.ds(0, half), pl.ds(0, lanes)] = causal
    bias_other[pl.ds(0, half), :] = causal
    for d in range(n):
        bias_early[pl.ds(d * half, half), pl.ds(lanes, lanes)] = blank
        bias_other[pl.ds((n + d) * half, half), :] = blank
        if d > 0:
            theirs = order[lax.rem(head + n - d, n) * m + blk]
            first = jnp.where(theirs < mine, 0.0, HIDDEN)
            bias_early[pl.ds(d * half, half), pl.ds(0, lanes)] = blank + first
            bias_other[pl.ds(d * half, half), :] = blank + (HIDDEN - first)

    def stacked(array, kv_head):
        cols = [pl.ds((kv_head * group + k) * HD, HD) for k in range(group)]
        return jnp.concatenate(
            [array[pl.ds(0, half), col] for col in cols]
            + [array[pl.ds(half, half), col] for col in cols],
            axis=0,
        )

    lo, hi = pl.ds(0, half), pl.ds(half, half)
    factor = scale * math.log2(math.e)

    def early_keys(i, cols):
        first = [kv[i, lo, cols]] + [part[d - 1, i, lo, cols] for d in range(1, n)]
        return jnp.concatenate(first, axis=0)

    def other_keys(i, cols):
        rest = [kv[i, hi, cols]] + [part[d - 1, i, hi, cols] for d in range(1, n)]
        rest += [early[d, i, :, cols] for d in range(n)]
        return jnp.concatenate(rest, axis=0)

    def first_logits(kv_head):
        cols = pl.ds(kv_head * HD, HD)
        logits = rows_dot(early_keys(0, cols), stacked(q, kv_head))
        ready[kv_head, 0] = logits * factor + bias_early[...]
        ready[kv_head, 1] = rows_dot(early_keys(1, cols), stacked(g, kv_head))

    def one_head(kv_head):
        cols = pl.ds(kv_head * HD, HD)
        key_first, key_rest = early_keys(0, cols), other_keys(0, cols)
        value_rest = other_keys(1, cols)
        queries, grads = stacked(q, kv_head), stacked(g, kv_head)
        late_queries, late_grads = queries[lanes:], grads[lanes:]
        logits_first, spread_first = ready[kv_head, 0], ready[kv_head, 1]
        logits_rest = rows_dot(key_rest, late_queries) * factor + bias_other[...]
        spread_rest = rows_dot(value_rest, late_grads)

        def both(reduce, combine, first, rest):
            whole = reduce(first, axis=0, keepdims=True)
            tail = combine(whole[:, lanes:], reduce(rest, axis=0, keepdims=True))
            return jnp.concatenate([whole[:, :lanes], tail], axis=1)

        top = both(jnp.max, jnp.maximum, logits_first, logits_rest)
        mass_first = jnp.exp2(logits_first - top)
        mass_rest = jnp.exp2(logits_rest - top[:, lanes:])
        inverse = 1.0 / both(jnp.sum, jnp.add, mass_first, mass_rest)
        weights_first = mass_first * inverse
        weights_rest = mass_rest * inverse[:, lanes:]
        delta = both(
            jnp.sum, jnp.add, weights_first * spread_first, weights_rest * spread_rest
        )
        slopes_first = (weights_first * (spread_first - delta)).astype(jnp.bfloat16)
        slopes_rest = (weights_rest * (spread_rest - delta[:, lanes:])).astype(jnp.bfloat16)
        weights_first = weights_first.astype(jnp.bfloat16)
        weights_rest = weights_rest.astype(jnp.bfloat16)

        query_first = cols_dot(slopes_first, key_first)
        query_rest = cols_dot(slopes_rest, key_rest)
        query_grad = (
            jnp.concatenate([query_first[:lanes], query_first[lanes:] + query_rest], axis=0)
            * scale
        ).astype(jnp.bfloat16)
        for k in range(group):
            out = pl.ds((kv_head * group + k) * HD, HD)
            dq[lo, out] = query_grad[k * half : (k + 1) * half]
            dq[hi, out] = query_grad[lanes + k * half : lanes + (k + 1) * half]
        grads_first = (
            plain_dot(slopes_first, queries) * scale,
            plain_dot(weights_first, grads),
        )
        grads_rest = (
            plain_dot(slopes_rest, late_queries) * scale,
            plain_dot(weights_rest, late_grads),
        )
        for i in range(2):
            own_grad[i, lo, cols] = grads_first[i][:half]
            own_grad[i, hi, cols] = grads_rest[i][:half]
            for d in range(1, n):
                at = d * half
                part_out[d - 1, i, lo, cols] = grads_first[i][at : at + half].astype(jnp.bfloat16)
                part_out[d - 1, i, hi, cols] = grads_rest[i][at : at + half].astype(jnp.bfloat16)
            for d in range(n):
                at = (n + d) * half
                prev_out[d, i, :, cols] = grads_rest[i][at : at + half].astype(jnp.bfloat16)

    def stage_arrive(c):
        for d in range(1, n):
            to_part(d, c, False).wait_recv()
            to_far(d, c).start()
            to_part(d, c, True).start()
        if c == 0:
            loads[2].wait()
            loads[3].wait()
        for index in range(heads_in):
            first_logits(c * heads_in + index)

    def stage_compute(c):
        to_near(c).wait_recv()
        for d in range(1, n):
            to_far(d, c).wait_recv()
            to_part(d, c, True).wait_recv()
        for index in range(heads_in):
            one_head(c * heads_in + index)
        to_prev(c).start()
        for d in range(1, n):
            to_late(d, c).start()
        dq_copy(c).start()

    def stage_front(c):
        to_prev(c).wait_recv()
        for d in range(1, n):
            for i in range(2):
                spot = (d - 1, i, pl.ds(0, half), span(c))
                total = part_out[spot].astype(jnp.float32)
                total = total + prev_in[d, i, :, span(c)].astype(jnp.float32)
                part_out[spot] = total.astype(jnp.bfloat16)
            to_front(d, c).start()

    def stage_finish(c):
        for d in range(1, n):
            to_late(d, c).wait_recv()
            to_front(d, c).wait_recv()
        for i in range(2):
            total = own_grad[i, :, span(c)]
            for d in range(1, n):
                total = total + part_in[d - 1, i, :, span(c)].astype(jnp.float32)
            front = total[:half] + prev_in[0, i, :, span(c)].astype(jnp.float32)
            result[i, pl.ds(0, half), span(c)] = front.astype(jnp.bfloat16)
            result[i, pl.ds(half, half), span(c)] = total[half:].astype(jnp.bfloat16)
            out_copy(i, c).start()

    for c in range(chunks):
        stage_arrive(c)
    for t in range(chunks + 2):
        if t < chunks:
            stage_compute(t)
        if t >= 2:
            stage_front(t - 2)
    for c in range(chunks):
        stage_finish(c)
    for c in range(chunks):
        to_near(c).wait_send()
        to_prev(c).wait_send()
        for d in range(1, n):
            to_part(d, c, False).wait_send()
            to_part(d, c, True).wait_send()
            to_far(d, c).wait_send()
            to_late(d, c).wait_send()
            to_front(d, c).wait_send()
        dq_copy(c).wait()
        out_copy(0, c).wait()
        out_copy(1, c).wait()


def hand_over(a, b, c, a_out, b_out, c_out, sem):
    rows = a.shape[0] // 4
    pairs = [(b, b_out), (c, c_out)]
    for i in range(4):
        pairs.append((a.at[pl.ds(i * rows, rows)], a_out.at[pl.ds(i * rows, rows)]))
    copies = [
        pltpu.make_async_copy(src, dst, sem.at[i]) for i, (src, dst) in enumerate(pairs)
    ]
    for copy in copies:
        copy.start()
    for copy in copies:
        copy.wait()


def solution(mesh):
    n, m = mesh.shape["head"], mesh.shape["blk"]

    def body(queries, keys, values, grad_out, order):
        rows, query_cols = queries.shape
        key_cols = keys.shape[1]
        half = rows // 2
        chunks = min(CHUNKS, key_cols // HD)
        lanes = half * (query_cols // key_cols)
        low, wide = jnp.bfloat16, jnp.float32
        dma = pltpu.SemaphoreType.DMA
        anywhere = pl.BlockSpec(memory_space=pl.ANY)
        grads = pl.pallas_call(
            functools.partial(kernel, n, m, order.shape[0], chunks),
            out_shape=(
                jax.ShapeDtypeStruct(queries.shape, low),
                jax.ShapeDtypeStruct(keys.shape, low),
                jax.ShapeDtypeStruct(values.shape, low),
            ),
            in_specs=[anywhere] * 5,
            out_specs=[anywhere] * 3,
            scratch_shapes=[
                pltpu.VMEM((rows, query_cols), low),
                pltpu.VMEM((rows, query_cols), low),
                pltpu.VMEM((rows, query_cols), low),
                pltpu.VMEM((2, rows, key_cols), low),
                pltpu.VMEM((n - 1, 2, rows, key_cols), low),
                pltpu.VMEM((n, 2, half, key_cols), low),
                pltpu.VMEM((2, rows, key_cols), wide),
                pltpu.VMEM((n, 2, half, key_cols), low),
                pltpu.VMEM((n, 2, half, key_cols), low),
                pltpu.VMEM((n - 1, 2, rows, key_cols), low),
                pltpu.VMEM((n - 1, 2, rows, key_cols), low),
                pltpu.VMEM((2, rows, key_cols), low),
                pltpu.VMEM((n * half, 2 * lanes), wide),
                pltpu.VMEM((2 * n * half, lanes), wide),
                pltpu.SMEM(order.shape, order.dtype),
                pltpu.VMEM((key_cols // HD, 2, n * half, 2 * lanes), wide),
                dma((5,)),
                dma((n - 1, chunks)), dma((n - 1, chunks)),
                dma((n - 1, chunks)), dma((n - 1, chunks)),
                dma((chunks,)), dma((chunks,)),
                dma((n - 1, chunks)), dma((n - 1, chunks)),
                dma((chunks,)), dma((chunks,)),
                dma((n - 1, chunks)), dma((n - 1, chunks)),
                dma((n - 1, chunks)), dma((n - 1, chunks)),
                dma((chunks,)), dma((2, chunks)),
            ],
            compiler_params=pltpu.CompilerParams(
                collective_id=0, has_side_effects=True, vmem_limit_bytes=40 * 2**20
            ),
        )(*(
            pltpu.with_memory_space_constraint(x, pltpu.HBM)
            for x in (order, queries, keys, values, grad_out)
        ))
        return pl.pallas_call(
            hand_over,
            out_shape=tuple(jax.ShapeDtypeStruct(x.shape, x.dtype) for x in grads),
            in_specs=[anywhere] * 3,
            out_specs=[anywhere] * 3,
            scratch_shapes=[dma((6,))],
            compiler_params=pltpu.CompilerParams(vmem_limit_bytes=2**20),
        )(*grads)

    shard = P(("head", "blk"), None)
    return jax.shard_map(
        body,
        mesh=mesh,
        in_specs=(shard, shard, shard, shard, P()),
        out_specs=(shard, shard, shard),
        check_vma=False,
    )
```

```python
import functools
import math

import jax
import jax.numpy as jnp
from jax import lax
from jax.experimental import pallas as pl
from jax.experimental.pallas import tpu as pltpu
from jax.sharding import PartitionSpec as P

MESH = pl.DeviceIdType.MESH
HD = 128
CHUNKS = 4
HIDDEN = -1e30


def rows_dot(left, right):
    return lax.dot_general(
        left, right, (((1,), (1,)), ((), ())), preferred_element_type=jnp.float32
    )


def plain_dot(left, right):
    return jnp.dot(left, right, preferred_element_type=jnp.float32)


def cols_dot(left, right):
    return lax.dot_general(
        left, right, (((0,), (0,)), ((), ())), preferred_element_type=jnp.float32
    )


def kernel(
    n, m, slots, chunks,
    order_hbm, q_hbm, k_hbm, v_hbm, g_hbm, dq_hbm, dk_hbm, dv_hbm,
    q, g, dq, kv, part, early, own_grad, prev_out, prev_in, part_out, part_in, result,
    bias_early, bias_other, order, ready,
    load_sem, head_s, head_r, tail_s, tail_r, near_s, near_r, far_s, far_r,
    prev_s, prev_r, late_s, late_r, front_s, front_r, dq_sem, out_sem,
):
    head, blk = lax.axis_index("head"), lax.axis_index("blk")
    rows, key_cols = kv.shape[1], kv.shape[2]
    half = rows // 2
    width = key_cols // chunks
    group = q.shape[1] // key_cols
    lanes = group * half
    heads_in = width // HD
    scale = HD ** -0.5
    ahead = (head, lax.rem(blk + 1, m))
    behind = (head, lax.rem(blk + m - 1, m))
    up = [None] + [(lax.rem(head + d, n), blk) for d in range(1, n)]
    down = [None] + [(lax.rem(head + n - d, n), blk) for d in range(1, n)]

    loads = [
        pltpu.make_async_copy(k_hbm, kv.at[0], load_sem.at[0]),
        pltpu.make_async_copy(v_hbm, kv.at[1], load_sem.at[1]),
        pltpu.make_async_copy(q_hbm, q, load_sem.at[2]),
        pltpu.make_async_copy(g_hbm, g, load_sem.at[3]),
        pltpu.make_async_copy(order_hbm, order, load_sem.at[4]),
    ]
    for load in loads:
        load.start()

    barrier = pltpu.get_barrier_semaphore()
    for other in up[1:] + [ahead, behind]:
        pl.semaphore_signal(barrier, inc=1, device_id=other, device_id_type=MESH)

    def span(c):
        return pl.ds(c * width, width)

    def remote(src, dst, send, recv, where):
        return pltpu.make_async_remote_copy(
            src_ref=src, dst_ref=dst, send_sem=send, recv_sem=recv,
            device_id=where, device_id_type=MESH,
        )

    def to_part(d, c, late):
        piece = (slice(None), pl.ds(half if late else 0, half), span(c))
        sends, recvs = (tail_s, tail_r) if late else (head_s, head_r)
        return remote(
            kv.at[piece], part.at[(d - 1,) + piece],
            sends.at[d - 1, c], recvs.at[d - 1, c], up[d],
        )

    def to_near(c):
        return remote(
            kv.at[:, pl.ds(0, half), span(c)], early.at[0, :, :, span(c)],
            near_s.at[c], near_r.at[c], ahead,
        )

    def to_far(d, c):
        return remote(
            part.at[d - 1, :, pl.ds(0, half), span(c)], early.at[d, :, :, span(c)],
            far_s.at[d - 1, c], far_r.at[d - 1, c], ahead,
        )

    def to_prev(c):
        return remote(
            prev_out.at[:, :, :, span(c)], prev_in.at[:, :, :, span(c)],
            prev_s.at[c], prev_r.at[c], behind,
        )

    def to_late(d, c):
        piece = (d - 1, slice(None), pl.ds(half, half), span(c))
        return remote(
            part_out.at[piece], part_in.at[piece],
            late_s.at[d - 1, c], late_r.at[d - 1, c], down[d],
        )

    def to_front(d, c):
        piece = (d - 1, slice(None), pl.ds(0, half), span(c))
        return remote(
            part_out.at[piece], part_in.at[piece],
            front_s.at[d - 1, c], front_r.at[d - 1, c], down[d],
        )

    def dq_copy(c):
        cols = pl.ds(c * width * group, width * group)
        return pltpu.make_async_copy(dq.at[:, cols], dq_hbm.at[:, cols], dq_sem.at[c])

    def out_copy(i, c):
        target = (dk_hbm, dv_hbm)[i]
        return pltpu.make_async_copy(
            result.at[i, :, span(c)], target.at[:, span(c)], out_sem.at[i, c]
        )

    loads[0].wait()
    loads[1].wait()
    pl.semaphore_wait(barrier, n + 1)
    for c in range(chunks):
        for d in range(1, n):
            to_part(d, c, False).start()
        to_near(c).start()
    for c in range(min(2, chunks)):
        for d in range(1, n):
            to_part(d, c, True).start()

    loads[4].wait()
    mine = order[head * m + blk]
    row = lax.broadcasted_iota(jnp.int32, (half, lanes), 0)
    col = lax.rem(lax.broadcasted_iota(jnp.int32, (half, lanes), 1), half)
    causal = jnp.where(row <= col, 0.0, HIDDEN)
    blank = jnp.zeros((half, lanes), jnp.float32)
    bias_early[pl.ds(0, half), pl.ds(0, lanes)] = causal
    bias_other[pl.ds(0, half), :] = causal
    for d in range(n):
        bias_early[pl.ds(d * half, half), pl.ds(lanes, lanes)] = blank
        bias_other[pl.ds((n + d) * half, half), :] = blank
        if d > 0:
            theirs = order[lax.rem(head + n - d, n) * m + blk]
            first = jnp.where(theirs < mine, 0.0, HIDDEN)
            bias_early[pl.ds(d * half, half), pl.ds(0, lanes)] = blank + first
            bias_other[pl.ds(d * half, half), :] = blank + (HIDDEN - first)

    def stacked(array, kv_head):
        cols = [pl.ds((kv_head * group + k) * HD, HD) for k in range(group)]
        return jnp.concatenate(
            [array[pl.ds(0, half), col] for col in cols]
            + [array[pl.ds(half, half), col] for col in cols],
            axis=0,
        )

    lo, hi = pl.ds(0, half), pl.ds(half, half)
    factor = scale * math.log2(math.e)

    def early_keys(i, cols):
        first = [kv[i, lo, cols]] + [part[d - 1, i, lo, cols] for d in range(1, n)]
        return jnp.concatenate(first, axis=0)

    def other_keys(i, cols):
        rest = [kv[i, hi, cols]] + [part[d - 1, i, hi, cols] for d in range(1, n)]
        rest += [early[d, i, :, cols] for d in range(n)]
        return jnp.concatenate(rest, axis=0)

    def first_logits(kv_head):
        cols = pl.ds(kv_head * HD, HD)
        logits = rows_dot(early_keys(0, cols), stacked(q, kv_head))
        ready[kv_head, 0] = logits * factor + bias_early[...]
        ready[kv_head, 1] = rows_dot(early_keys(1, cols), stacked(g, kv_head))

    def one_head(kv_head):
        cols = pl.ds(kv_head * HD, HD)
        key_first, key_rest = early_keys(0, cols), other_keys(0, cols)
        value_rest = other_keys(1, cols)
        queries, grads = stacked(q, kv_head), stacked(g, kv_head)
        late_queries, late_grads = queries[lanes:], grads[lanes:]
        logits_first, spread_first = ready[kv_head, 0], ready[kv_head, 1]
        logits_rest = rows_dot(key_rest, late_queries) * factor + bias_other[...]
        spread_rest = rows_dot(value_rest, late_grads)

        def both(reduce, combine, first, rest):
            whole = reduce(first, axis=0, keepdims=True)
            tail = combine(whole[:, lanes:], reduce(rest, axis=0, keepdims=True))
            return jnp.concatenate([whole[:, :lanes], tail], axis=1)

        top = both(jnp.max, jnp.maximum, logits_first, logits_rest)
        mass_first = jnp.exp2(logits_first - top)
        mass_rest = jnp.exp2(logits_rest - top[:, lanes:])
        inverse = 1.0 / both(jnp.sum, jnp.add, mass_first, mass_rest)
        weights_first = mass_first * inverse
        weights_rest = mass_rest * inverse[:, lanes:]
        delta = both(
            jnp.sum, jnp.add, weights_first * spread_first, weights_rest * spread_rest
        )
        slopes_first = (weights_first * (spread_first - delta)).astype(jnp.bfloat16)
        slopes_rest = (weights_rest * (spread_rest - delta[:, lanes:])).astype(jnp.bfloat16)
        weights_first = weights_first.astype(jnp.bfloat16)
        weights_rest = weights_rest.astype(jnp.bfloat16)

        query_first = cols_dot(slopes_first, key_first)
        query_rest = cols_dot(slopes_rest, key_rest)
        query_grad = (
            jnp.concatenate([query_first[:lanes], query_first[lanes:] + query_rest], axis=0)
            * scale
        ).astype(jnp.bfloat16)
        for k in range(group):
            out = pl.ds((kv_head * group + k) * HD, HD)
            dq[lo, out] = query_grad[k * half : (k + 1) * half]
            dq[hi, out] = query_grad[lanes + k * half : lanes + (k + 1) * half]
        grads_first = (
            plain_dot(slopes_first, queries) * scale,
            plain_dot(weights_first, grads),
        )
        grads_rest = (
            plain_dot(slopes_rest, late_queries) * scale,
            plain_dot(weights_rest, late_grads),
        )
        for i in range(2):
            own_grad[i, lo, cols] = grads_first[i][:half]
            own_grad[i, hi, cols] = grads_rest[i][:half]
            for d in range(1, n):
                at = d * half
                part_out[d - 1, i, lo, cols] = grads_first[i][at : at + half].astype(jnp.bfloat16)
                part_out[d - 1, i, hi, cols] = grads_rest[i][at : at + half].astype(jnp.bfloat16)
            for d in range(n):
                at = (n + d) * half
                prev_out[d, i, :, cols] = grads_rest[i][at : at + half].astype(jnp.bfloat16)

    def stage_arrive(c):
        for d in range(1, n):
            to_part(d, c, False).wait_recv()
            to_far(d, c).start()
            if c + 2 < chunks:
                to_part(d, c + 2, True).start()
        if c == 0:
            loads[2].wait()
            loads[3].wait()
        for index in range(heads_in):
            first_logits(c * heads_in + index)

    def stage_compute(c):
        to_near(c).wait_recv()
        for d in range(1, n):
            to_far(d, c).wait_recv()
            to_part(d, c, True).wait_recv()
        for index in range(heads_in):
            one_head(c * heads_in + index)
        to_prev(c).start()
        for d in range(1, n):
            to_late(d, c).start()
        dq_copy(c).start()

    def stage_front(c):
        to_prev(c).wait_recv()
        for d in range(1, n):
            for i in range(2):
                spot = (d - 1, i, pl.ds(0, half), span(c))
                total = part_out[spot].astype(jnp.float32)
                total = total + prev_in[d, i, :, span(c)].astype(jnp.float32)
                part_out[spot] = total.astype(jnp.bfloat16)
            to_front(d, c).start()

    def stage_finish(c):
        for d in range(1, n):
            to_late(d, c).wait_recv()
            to_front(d, c).wait_recv()
        for i in range(2):
            total = own_grad[i, :, span(c)]
            for d in range(1, n):
                total = total + part_in[d - 1, i, :, span(c)].astype(jnp.float32)
            front = total[:half] + prev_in[0, i, :, span(c)].astype(jnp.float32)
            result[i, pl.ds(0, half), span(c)] = front.astype(jnp.bfloat16)
            result[i, pl.ds(half, half), span(c)] = total[half:].astype(jnp.bfloat16)
            out_copy(i, c).start()

    for c in range(chunks):
        stage_arrive(c)
    for t in range(chunks + 2):
        if t < chunks:
            stage_compute(t)
        if t >= 2:
            stage_front(t - 2)
    for c in range(chunks):
        stage_finish(c)
    for c in range(chunks):
        to_near(c).wait_send()
        to_prev(c).wait_send()
        for d in range(1, n):
            to_part(d, c, False).wait_send()
            to_part(d, c, True).wait_send()
            to_far(d, c).wait_send()
            to_late(d, c).wait_send()
            to_front(d, c).wait_send()
        dq_copy(c).wait()
        out_copy(0, c).wait()
        out_copy(1, c).wait()


def hand_over(a, b, c, a_out, b_out, c_out, sem):
    rows = a.shape[0] // 4
    pairs = [(b, b_out), (c, c_out)]
    for i in range(4):
        pairs.append((a.at[pl.ds(i * rows, rows)], a_out.at[pl.ds(i * rows, rows)]))
    copies = [
        pltpu.make_async_copy(src, dst, sem.at[i]) for i, (src, dst) in enumerate(pairs)
    ]
    for copy in copies:
        copy.start()
    for copy in copies:
        copy.wait()


def solution(mesh):
    n, m = mesh.shape["head"], mesh.shape["blk"]

    def body(queries, keys, values, grad_out, order):
        rows, query_cols = queries.shape
        key_cols = keys.shape[1]
        half = rows // 2
        chunks = min(CHUNKS, key_cols // HD)
        lanes = half * (query_cols // key_cols)
        low, wide = jnp.bfloat16, jnp.float32
        dma = pltpu.SemaphoreType.DMA
        anywhere = pl.BlockSpec(memory_space=pl.ANY)
        grads = pl.pallas_call(
            functools.partial(kernel, n, m, order.shape[0], chunks),
            out_shape=(
                jax.ShapeDtypeStruct(queries.shape, low),
                jax.ShapeDtypeStruct(keys.shape, low),
                jax.ShapeDtypeStruct(values.shape, low),
            ),
            in_specs=[anywhere] * 5,
            out_specs=[anywhere] * 3,
            scratch_shapes=[
                pltpu.VMEM((rows, query_cols), low),
                pltpu.VMEM((rows, query_cols), low),
                pltpu.VMEM((rows, query_cols), low),
                pltpu.VMEM((2, rows, key_cols), low),
                pltpu.VMEM((n - 1, 2, rows, key_cols), low),
                pltpu.VMEM((n, 2, half, key_cols), low),
                pltpu.VMEM((2, rows, key_cols), wide),
                pltpu.VMEM((n, 2, half, key_cols), low),
                pltpu.VMEM((n, 2, half, key_cols), low),
                pltpu.VMEM((n - 1, 2, rows, key_cols), low),
                pltpu.VMEM((n - 1, 2, rows, key_cols), low),
                pltpu.VMEM((2, rows, key_cols), low),
                pltpu.VMEM((n * half, 2 * lanes), wide),
                pltpu.VMEM((2 * n * half, lanes), wide),
                pltpu.SMEM(order.shape, order.dtype),
                pltpu.VMEM((key_cols // HD, 2, n * half, 2 * lanes), wide),
                dma((5,)),
                dma((n - 1, chunks)), dma((n - 1, chunks)),
                dma((n - 1, chunks)), dma((n - 1, chunks)),
                dma((chunks,)), dma((chunks,)),
                dma((n - 1, chunks)), dma((n - 1, chunks)),
                dma((chunks,)), dma((chunks,)),
                dma((n - 1, chunks)), dma((n - 1, chunks)),
                dma((n - 1, chunks)), dma((n - 1, chunks)),
                dma((chunks,)), dma((2, chunks)),
            ],
            compiler_params=pltpu.CompilerParams(
                collective_id=0, has_side_effects=True, vmem_limit_bytes=40 * 2**20
            ),
        )(*(
            pltpu.with_memory_space_constraint(x, pltpu.HBM)
            for x in (order, queries, keys, values, grad_out)
        ))
        return pl.pallas_call(
            hand_over,
            out_shape=tuple(jax.ShapeDtypeStruct(x.shape, x.dtype) for x in grads),
            in_specs=[anywhere] * 3,
            out_specs=[anywhere] * 3,
            scratch_shapes=[dma((6,))],
            compiler_params=pltpu.CompilerParams(vmem_limit_bytes=2**20),
        )(*grads)

    shard = P(("head", "blk"), None)
    return jax.shard_map(
        body,
        mesh=mesh,
        in_specs=(shard, shard, shard, shard, P()),
        out_specs=(shard, shard, shard),
        check_vma=False,
    )
```

```python
import functools
import math

import jax
import jax.numpy as jnp
from jax import lax
from jax.experimental import pallas as pl
from jax.experimental.pallas import tpu as pltpu
from jax.sharding import PartitionSpec as P

MESH = pl.DeviceIdType.MESH
HD = 128
CHUNKS = 4
HIDDEN = -1e30


def rows_dot(left, right):
    return lax.dot_general(
        left, right, (((1,), (1,)), ((), ())), preferred_element_type=jnp.float32
    )


def plain_dot(left, right):
    return jnp.dot(left, right, preferred_element_type=jnp.float32)


def cols_dot(left, right):
    return lax.dot_general(
        left, right, (((0,), (0,)), ((), ())), preferred_element_type=jnp.float32
    )


def kernel(
    n, m, slots, chunks,
    order_hbm, q_hbm, k_hbm, v_hbm, g_hbm, dq_hbm, dk_hbm, dv_hbm,
    q, g, dq, kv, part, early, own_grad, prev_out, prev_in, part_out, part_in, result,
    bias_early, bias_other, order, ready,
    load_sem, head_s, head_r, tail_s, tail_r, near_s, near_r, far_s, far_r,
    prev_s, prev_r, late_s, late_r, front_s, front_r, dq_sem, out_sem,
):
    head, blk = lax.axis_index("head"), lax.axis_index("blk")
    rows, key_cols = kv.shape[1], kv.shape[2]
    half = rows // 2
    width = key_cols // chunks
    group = q.shape[1] // key_cols
    lanes = group * half
    heads_in = width // HD
    scale = HD ** -0.5
    ahead = (head, lax.rem(blk + 1, m))
    behind = (head, lax.rem(blk + m - 1, m))
    up = [None] + [(lax.rem(head + d, n), blk) for d in range(1, n)]
    down = [None] + [(lax.rem(head + n - d, n), blk) for d in range(1, n)]

    loads = [
        pltpu.make_async_copy(k_hbm, kv.at[0], load_sem.at[0]),
        pltpu.make_async_copy(v_hbm, kv.at[1], load_sem.at[1]),
        pltpu.make_async_copy(q_hbm, q, load_sem.at[2]),
        pltpu.make_async_copy(g_hbm, g, load_sem.at[3]),
        pltpu.make_async_copy(order_hbm, order, load_sem.at[4]),
    ]
    for load in loads:
        load.start()

    barrier = pltpu.get_barrier_semaphore()
    for other in up[1:] + [ahead, behind]:
        pl.semaphore_signal(barrier, inc=1, device_id=other, device_id_type=MESH)

    def span(c):
        return pl.ds(c * width, width)

    def remote(src, dst, send, recv, where):
        return pltpu.make_async_remote_copy(
            src_ref=src, dst_ref=dst, send_sem=send, recv_sem=recv,
            device_id=where, device_id_type=MESH,
        )

    def to_part(d, c, late):
        piece = (slice(None), pl.ds(half if late else 0, half), span(c))
        sends, recvs = (tail_s, tail_r) if late else (head_s, head_r)
        return remote(
            kv.at[piece], part.at[(d - 1,) + piece],
            sends.at[d - 1, c], recvs.at[d - 1, c], up[d],
        )

    def to_near(c):
        return remote(
            kv.at[:, pl.ds(0, half), span(c)], early.at[0, :, :, span(c)],
            near_s.at[c], near_r.at[c], ahead,
        )

    def to_far(d, c):
        return remote(
            part.at[d - 1, :, pl.ds(0, half), span(c)], early.at[d, :, :, span(c)],
            far_s.at[d - 1, c], far_r.at[d - 1, c], ahead,
        )

    def to_prev(c):
        return remote(
            prev_out.at[:, :, :, span(c)], prev_in.at[:, :, :, span(c)],
            prev_s.at[c], prev_r.at[c], behind,
        )

    def to_late(d, c):
        piece = (d - 1, slice(None), pl.ds(half, half), span(c))
        return remote(
            part_out.at[piece], part_in.at[piece],
            late_s.at[d - 1, c], late_r.at[d - 1, c], down[d],
        )

    def to_front(d, c):
        piece = (d - 1, slice(None), pl.ds(0, half), span(c))
        return remote(
            part_out.at[piece], part_in.at[piece],
            front_s.at[d - 1, c], front_r.at[d - 1, c], down[d],
        )

    def dq_copy(c):
        cols = pl.ds(c * width * group, width * group)
        return pltpu.make_async_copy(dq.at[:, cols], dq_hbm.at[:, cols], dq_sem.at[c])

    def out_copy(i, c):
        target = (dk_hbm, dv_hbm)[i]
        return pltpu.make_async_copy(
            result.at[i, :, span(c)], target.at[:, span(c)], out_sem.at[i, c]
        )

    loads[0].wait()
    loads[1].wait()
    pl.semaphore_wait(barrier, n + 1)
    for c in range(chunks):
        for d in range(1, n):
            to_part(d, c, False).start()
        to_near(c).start()
    for c in range(min(2, chunks)):
        for d in range(1, n):
            to_part(d, c, True).start()

    loads[4].wait()
    mine = order[head * m + blk]
    row = lax.broadcasted_iota(jnp.int32, (half, lanes), 0)
    col = lax.rem(lax.broadcasted_iota(jnp.int32, (half, lanes), 1), half)
    causal = jnp.where(row <= col, 0.0, HIDDEN)
    blank = jnp.zeros((half, lanes), jnp.float32)
    bias_early[pl.ds(0, half), pl.ds(0, lanes)] = causal
    bias_other[pl.ds(0, half), :] = causal
    for d in range(n):
        bias_early[pl.ds(d * half, half), pl.ds(lanes, lanes)] = blank
        bias_other[pl.ds((n + d) * half, half), :] = blank
        if d > 0:
            theirs = order[lax.rem(head + n - d, n) * m + blk]
            first = jnp.where(theirs < mine, 0.0, HIDDEN)
            bias_early[pl.ds(d * half, half), pl.ds(0, lanes)] = blank + first
            bias_other[pl.ds(d * half, half), :] = blank + (HIDDEN - first)

    def stacked(array, kv_head):
        cols = [pl.ds((kv_head * group + k) * HD, HD) for k in range(group)]
        return jnp.concatenate(
            [array[pl.ds(0, half), col] for col in cols]
            + [array[pl.ds(half, half), col] for col in cols],
            axis=0,
        )

    lo, hi = pl.ds(0, half), pl.ds(half, half)
    factor = scale * math.log2(math.e)

    def early_keys(i, cols):
        first = [kv[i, lo, cols]] + [part[d - 1, i, lo, cols] for d in range(1, n)]
        return jnp.concatenate(first, axis=0)

    def other_keys(i, cols):
        rest = [kv[i, hi, cols]] + [part[d - 1, i, hi, cols] for d in range(1, n)]
        rest += [early[d, i, :, cols] for d in range(n)]
        return jnp.concatenate(rest, axis=0)

    def first_logits(kv_head):
        cols = pl.ds(kv_head * HD, HD)
        logits = rows_dot(early_keys(0, cols), stacked(q, kv_head))
        ready[kv_head, 0] = logits * factor + bias_early[...]
        ready[kv_head, 1] = rows_dot(early_keys(1, cols), stacked(g, kv_head))

    def one_head(kv_head):
        cols = pl.ds(kv_head * HD, HD)
        key_first, key_rest = early_keys(0, cols), other_keys(0, cols)
        value_rest = other_keys(1, cols)
        queries, grads = stacked(q, kv_head), stacked(g, kv_head)
        late_queries, late_grads = queries[lanes:], grads[lanes:]
        logits_first, spread_first = ready[kv_head, 0], ready[kv_head, 1]
        logits_rest = rows_dot(key_rest, late_queries) * factor + bias_other[...]
        spread_rest = rows_dot(value_rest, late_grads)

        def both(reduce, combine, first, rest):
            whole = reduce(first, axis=0, keepdims=True)
            tail = combine(whole[:, lanes:], reduce(rest, axis=0, keepdims=True))
            return jnp.concatenate([whole[:, :lanes], tail], axis=1)

        top = both(jnp.max, jnp.maximum, logits_first, logits_rest)
        mass_first = jnp.exp2(logits_first - top)
        mass_rest = jnp.exp2(logits_rest - top[:, lanes:])
        inverse = 1.0 / both(jnp.sum, jnp.add, mass_first, mass_rest)
        weights_first = mass_first * inverse
        weights_rest = mass_rest * inverse[:, lanes:]
        delta = both(
            jnp.sum, jnp.add, weights_first * spread_first, weights_rest * spread_rest
        )
        slopes_first = (weights_first * (spread_first - delta)).astype(jnp.bfloat16)
        slopes_rest = (weights_rest * (spread_rest - delta[:, lanes:])).astype(jnp.bfloat16)
        weights_first = weights_first.astype(jnp.bfloat16)
        weights_rest = weights_rest.astype(jnp.bfloat16)

        grads_first = (
            plain_dot(slopes_first, queries) * scale,
            plain_dot(weights_first, grads),
        )
        grads_rest = (
            plain_dot(slopes_rest, late_queries) * scale,
            plain_dot(weights_rest, late_grads),
        )
        for i in range(2):
            own_grad[i, lo, cols] = grads_first[i][:half]
            own_grad[i, hi, cols] = grads_rest[i][:half]
            for d in range(1, n):
                at = d * half
                part_out[d - 1, i, lo, cols] = grads_first[i][at : at + half].astype(jnp.bfloat16)
                part_out[d - 1, i, hi, cols] = grads_rest[i][at : at + half].astype(jnp.bfloat16)
            for d in range(n):
                at = (n + d) * half
                prev_out[d, i, :, cols] = grads_rest[i][at : at + half].astype(jnp.bfloat16)

        def query_side():
            query_first = cols_dot(slopes_first, key_first)
            query_rest = cols_dot(slopes_rest, key_rest)
            query_grad = (
                jnp.concatenate([query_first[:lanes], query_first[lanes:] + query_rest], axis=0)
                * scale
            ).astype(jnp.bfloat16)
            for k in range(group):
                out = pl.ds((kv_head * group + k) * HD, HD)
                dq[lo, out] = query_grad[k * half : (k + 1) * half]
                dq[hi, out] = query_grad[lanes + k * half : lanes + (k + 1) * half]

        return query_side

    def stage_arrive(c):
        for d in range(1, n):
            to_part(d, c, False).wait_recv()
            to_far(d, c).start()
            if c + 2 < chunks:
                to_part(d, c + 2, True).start()
        if c == 0:
            loads[2].wait()
            loads[3].wait()
        for index in range(heads_in):
            first_logits(c * heads_in + index)

    def stage_compute(c):
        to_near(c).wait_recv()
        for d in range(1, n):
            to_far(d, c).wait_recv()
            to_part(d, c, True).wait_recv()
        query_sides = [one_head(c * heads_in + index) for index in range(heads_in)]
        to_prev(c).start()
        for d in range(1, n):
            to_late(d, c).start()
        for query_side in query_sides:
            query_side()
        dq_copy(c).start()

    def stage_front(c):
        to_prev(c).wait_recv()
        for d in range(1, n):
            for i in range(2):
                spot = (d - 1, i, pl.ds(0, half), span(c))
                total = part_out[spot].astype(jnp.float32)
                total = total + prev_in[d, i, :, span(c)].astype(jnp.float32)
                part_out[spot] = total.astype(jnp.bfloat16)
            to_front(d, c).start()

    def stage_finish(c):
        for d in range(1, n):
            to_late(d, c).wait_recv()
            to_front(d, c).wait_recv()
        for i in range(2):
            total = own_grad[i, :, span(c)]
            for d in range(1, n):
                total = total + part_in[d - 1, i, :, span(c)].astype(jnp.float32)
            front = total[:half] + prev_in[0, i, :, span(c)].astype(jnp.float32)
            result[i, pl.ds(0, half), span(c)] = front.astype(jnp.bfloat16)
            result[i, pl.ds(half, half), span(c)] = total[half:].astype(jnp.bfloat16)
            out_copy(i, c).start()

    for c in range(chunks):
        stage_arrive(c)
    for t in range(chunks + 2):
        if t < chunks:
            stage_compute(t)
        if t >= 2:
            stage_front(t - 2)
    for c in range(chunks):
        stage_finish(c)
    for c in range(chunks):
        to_near(c).wait_send()
        to_prev(c).wait_send()
        for d in range(1, n):
            to_part(d, c, False).wait_send()
            to_part(d, c, True).wait_send()
            to_far(d, c).wait_send()
            to_late(d, c).wait_send()
            to_front(d, c).wait_send()
        dq_copy(c).wait()
        out_copy(0, c).wait()
        out_copy(1, c).wait()


def hand_over(a, b, c, a_out, b_out, c_out, sem):
    rows = a.shape[0] // 4
    pairs = [(b, b_out), (c, c_out)]
    for i in range(4):
        pairs.append((a.at[pl.ds(i * rows, rows)], a_out.at[pl.ds(i * rows, rows)]))
    copies = [
        pltpu.make_async_copy(src, dst, sem.at[i]) for i, (src, dst) in enumerate(pairs)
    ]
    for copy in copies:
        copy.start()
    for copy in copies:
        copy.wait()


def solution(mesh):
    n, m = mesh.shape["head"], mesh.shape["blk"]

    def body(queries, keys, values, grad_out, order):
        rows, query_cols = queries.shape
        key_cols = keys.shape[1]
        half = rows // 2
        chunks = min(CHUNKS, key_cols // HD)
        lanes = half * (query_cols // key_cols)
        low, wide = jnp.bfloat16, jnp.float32
        dma = pltpu.SemaphoreType.DMA
        anywhere = pl.BlockSpec(memory_space=pl.ANY)
        grads = pl.pallas_call(
            functools.partial(kernel, n, m, order.shape[0], chunks),
            out_shape=(
                jax.ShapeDtypeStruct(queries.shape, low),
                jax.ShapeDtypeStruct(keys.shape, low),
                jax.ShapeDtypeStruct(values.shape, low),
            ),
            in_specs=[anywhere] * 5,
            out_specs=[anywhere] * 3,
            scratch_shapes=[
                pltpu.VMEM((rows, query_cols), low),
                pltpu.VMEM((rows, query_cols), low),
                pltpu.VMEM((rows, query_cols), low),
                pltpu.VMEM((2, rows, key_cols), low),
                pltpu.VMEM((n - 1, 2, rows, key_cols), low),
                pltpu.VMEM((n, 2, half, key_cols), low),
                pltpu.VMEM((2, rows, key_cols), wide),
                pltpu.VMEM((n, 2, half, key_cols), low),
                pltpu.VMEM((n, 2, half, key_cols), low),
                pltpu.VMEM((n - 1, 2, rows, key_cols), low),
                pltpu.VMEM((n - 1, 2, rows, key_cols), low),
                pltpu.VMEM((2, rows, key_cols), low),
                pltpu.VMEM((n * half, 2 * lanes), wide),
                pltpu.VMEM((2 * n * half, lanes), wide),
                pltpu.SMEM(order.shape, order.dtype),
                pltpu.VMEM((key_cols // HD, 2, n * half, 2 * lanes), wide),
                dma((5,)),
                dma((n - 1, chunks)), dma((n - 1, chunks)),
                dma((n - 1, chunks)), dma((n - 1, chunks)),
                dma((chunks,)), dma((chunks,)),
                dma((n - 1, chunks)), dma((n - 1, chunks)),
                dma((chunks,)), dma((chunks,)),
                dma((n - 1, chunks)), dma((n - 1, chunks)),
                dma((n - 1, chunks)), dma((n - 1, chunks)),
                dma((chunks,)), dma((2, chunks)),
            ],
            compiler_params=pltpu.CompilerParams(
                collective_id=0, has_side_effects=True, vmem_limit_bytes=40 * 2**20
            ),
        )(*(
            pltpu.with_memory_space_constraint(x, pltpu.HBM)
            for x in (order, queries, keys, values, grad_out)
        ))
        return pl.pallas_call(
            hand_over,
            out_shape=tuple(jax.ShapeDtypeStruct(x.shape, x.dtype) for x in grads),
            in_specs=[anywhere] * 3,
            out_specs=[anywhere] * 3,
            scratch_shapes=[dma((6,))],
            compiler_params=pltpu.CompilerParams(vmem_limit_bytes=2**20),
        )(*grads)

    shard = P(("head", "blk"), None)
    return jax.shard_map(
        body,
        mesh=mesh,
        in_specs=(shard, shard, shard, shard, P()),
        out_specs=(shard, shard, shard),
        check_vma=False,
    )
```

```python
import functools
import math

import jax
import jax.numpy as jnp
from jax import lax
from jax.experimental import pallas as pl
from jax.experimental.pallas import tpu as pltpu
from jax.sharding import PartitionSpec as P

MESH = pl.DeviceIdType.MESH
HD = 128
CHUNKS = 4
HIDDEN = -1e30


def rows_dot(left, right):
    return lax.dot_general(
        left, right, (((1,), (1,)), ((), ())), preferred_element_type=jnp.float32
    )


def plain_dot(left, right):
    return jnp.dot(left, right, preferred_element_type=jnp.float32)


def cols_dot(left, right):
    return lax.dot_general(
        left, right, (((0,), (0,)), ((), ())), preferred_element_type=jnp.float32
    )


def kernel(
    n, m, slots, chunks,
    order_hbm, q_hbm, k_hbm, v_hbm, g_hbm, dq_hbm, dk_hbm, dv_hbm,
    q, g, dq, kv, part, early, own_grad, prev_out, prev_in, part_out, part_in, result,
    bias_early, bias_other, order, ready,
    load_sem, head_s, head_r, tail_s, tail_r, near_s, near_r, far_s, far_r,
    prev_s, prev_r, late_s, late_r, front_s, front_r, dq_sem, out_sem,
):
    head, blk = lax.axis_index("head"), lax.axis_index("blk")
    rows, key_cols = kv.shape[1], kv.shape[2]
    half = rows // 2
    width = key_cols // chunks
    group = q.shape[1] // key_cols
    lanes = group * half
    heads_in = width // HD
    scale = HD ** -0.5
    ahead = (head, lax.rem(blk + 1, m))
    behind = (head, lax.rem(blk + m - 1, m))
    up = [None] + [(lax.rem(head + d, n), blk) for d in range(1, n)]
    down = [None] + [(lax.rem(head + n - d, n), blk) for d in range(1, n)]

    loads = [
        pltpu.make_async_copy(k_hbm, kv.at[0], load_sem.at[0]),
        pltpu.make_async_copy(v_hbm, kv.at[1], load_sem.at[1]),
        pltpu.make_async_copy(q_hbm, q, load_sem.at[2]),
        pltpu.make_async_copy(g_hbm, g, load_sem.at[3]),
        pltpu.make_async_copy(order_hbm, order, load_sem.at[4]),
    ]
    for load in loads:
        load.start()

    barrier = pltpu.get_barrier_semaphore()
    for other in up[1:] + [ahead, behind]:
        pl.semaphore_signal(barrier, inc=1, device_id=other, device_id_type=MESH)

    def span(c):
        return pl.ds(c * width, width)

    def remote(src, dst, send, recv, where):
        return pltpu.make_async_remote_copy(
            src_ref=src, dst_ref=dst, send_sem=send, recv_sem=recv,
            device_id=where, device_id_type=MESH,
        )

    def to_part(d, c, late):
        piece = (slice(None), pl.ds(half if late else 0, half), span(c))
        sends, recvs = (tail_s, tail_r) if late else (head_s, head_r)
        return remote(
            kv.at[piece], part.at[(d - 1,) + piece],
            sends.at[d - 1, c], recvs.at[d - 1, c], up[d],
        )

    def to_near():
        return remote(
            kv.at[:, pl.ds(0, half)], early.at[0], near_s.at[0], near_r.at[0], ahead
        )

    def to_far(d, c):
        return remote(
            part.at[d - 1, :, pl.ds(0, half), span(c)], early.at[d, :, :, span(c)],
            far_s.at[d - 1, c], far_r.at[d - 1, c], ahead,
        )

    def to_prev(c):
        return remote(
            prev_out.at[:, :, :, span(c)], prev_in.at[:, :, :, span(c)],
            prev_s.at[c], prev_r.at[c], behind,
        )

    def to_late(d, c):
        piece = (d - 1, slice(None), pl.ds(half, half), span(c))
        return remote(
            part_out.at[piece], part_in.at[piece],
            late_s.at[d - 1, c], late_r.at[d - 1, c], down[d],
        )

    def to_front(d, c):
        piece = (d - 1, slice(None), pl.ds(0, half), span(c))
        return remote(
            part_out.at[piece], part_in.at[piece],
            front_s.at[d - 1, c], front_r.at[d - 1, c], down[d],
        )

    def dq_copy(c):
        cols = pl.ds(c * width * group, width * group)
        return pltpu.make_async_copy(dq.at[:, cols], dq_hbm.at[:, cols], dq_sem.at[c])

    def out_copy(i, c):
        target = (dk_hbm, dv_hbm)[i]
        return pltpu.make_async_copy(
            result.at[i, :, span(c)], target.at[:, span(c)], out_sem.at[i, c]
        )

    loads[0].wait()
    loads[1].wait()
    pl.semaphore_wait(barrier, n + 1)
    for c in range(chunks):
        for d in range(1, n):
            to_part(d, c, False).start()
        if c == 0:
            to_near().start()
    for c in range(min(2, chunks)):
        for d in range(1, n):
            to_part(d, c, True).start()

    loads[4].wait()
    mine = order[head * m + blk]
    row = lax.broadcasted_iota(jnp.int32, (half, lanes), 0)
    col = lax.rem(lax.broadcasted_iota(jnp.int32, (half, lanes), 1), half)
    causal = jnp.where(row <= col, 0.0, HIDDEN)
    blank = jnp.zeros((half, lanes), jnp.float32)
    bias_early[pl.ds(0, half), pl.ds(0, lanes)] = causal
    bias_other[pl.ds(0, half), :] = causal
    for d in range(n):
        bias_early[pl.ds(d * half, half), pl.ds(lanes, lanes)] = blank
        bias_other[pl.ds((n + d) * half, half), :] = blank
        if d > 0:
            theirs = order[lax.rem(head + n - d, n) * m + blk]
            first = jnp.where(theirs < mine, 0.0, HIDDEN)
            bias_early[pl.ds(d * half, half), pl.ds(0, lanes)] = blank + first
            bias_other[pl.ds(d * half, half), :] = blank + (HIDDEN - first)

    def stacked(array, kv_head):
        cols = [pl.ds((kv_head * group + k) * HD, HD) for k in range(group)]
        return jnp.concatenate(
            [array[pl.ds(0, half), col] for col in cols]
            + [array[pl.ds(half, half), col] for col in cols],
            axis=0,
        )

    lo, hi = pl.ds(0, half), pl.ds(half, half)
    factor = scale * math.log2(math.e)

    def early_keys(i, cols):
        first = [kv[i, lo, cols]] + [part[d - 1, i, lo, cols] for d in range(1, n)]
        return jnp.concatenate(first, axis=0)

    def other_keys(i, cols):
        rest = [kv[i, hi, cols]] + [part[d - 1, i, hi, cols] for d in range(1, n)]
        rest += [early[d, i, :, cols] for d in range(n)]
        return jnp.concatenate(rest, axis=0)

    def first_logits(kv_head):
        cols = pl.ds(kv_head * HD, HD)
        logits = rows_dot(early_keys(0, cols), stacked(q, kv_head))
        ready[kv_head, 0] = logits * factor + bias_early[...]
        ready[kv_head, 1] = rows_dot(early_keys(1, cols), stacked(g, kv_head))

    def one_head(kv_head):
        cols = pl.ds(kv_head * HD, HD)
        key_first, key_rest = early_keys(0, cols), other_keys(0, cols)
        value_rest = other_keys(1, cols)
        queries, grads = stacked(q, kv_head), stacked(g, kv_head)
        late_queries, late_grads = queries[lanes:], grads[lanes:]
        logits_first, spread_first = ready[kv_head, 0], ready[kv_head, 1]
        logits_rest = rows_dot(key_rest, late_queries) * factor + bias_other[...]
        spread_rest = rows_dot(value_rest, late_grads)

        def both(reduce, combine, first, rest):
            whole = reduce(first, axis=0, keepdims=True)
            tail = combine(whole[:, lanes:], reduce(rest, axis=0, keepdims=True))
            return jnp.concatenate([whole[:, :lanes], tail], axis=1)

        top = both(jnp.max, jnp.maximum, logits_first, logits_rest)
        mass_first = jnp.exp2(logits_first - top)
        mass_rest = jnp.exp2(logits_rest - top[:, lanes:])
        inverse = 1.0 / both(jnp.sum, jnp.add, mass_first, mass_rest)
        weights_first = mass_first * inverse
        weights_rest = mass_rest * inverse[:, lanes:]
        delta = both(
            jnp.sum, jnp.add, weights_first * spread_first, weights_rest * spread_rest
        )
        slopes_first = (weights_first * (spread_first - delta)).astype(jnp.bfloat16)
        slopes_rest = (weights_rest * (spread_rest - delta[:, lanes:])).astype(jnp.bfloat16)
        weights_first = weights_first.astype(jnp.bfloat16)
        weights_rest = weights_rest.astype(jnp.bfloat16)

        grads_first = (
            plain_dot(slopes_first, queries) * scale,
            plain_dot(weights_first, grads),
        )
        grads_rest = (
            plain_dot(slopes_rest, late_queries) * scale,
            plain_dot(weights_rest, late_grads),
        )
        for i in range(2):
            own_grad[i, lo, cols] = grads_first[i][:half]
            own_grad[i, hi, cols] = grads_rest[i][:half]
            for d in range(1, n):
                at = d * half
                part_out[d - 1, i, lo, cols] = grads_first[i][at : at + half].astype(jnp.bfloat16)
                part_out[d - 1, i, hi, cols] = grads_rest[i][at : at + half].astype(jnp.bfloat16)
            for d in range(n):
                at = (n + d) * half
                prev_out[d, i, :, cols] = grads_rest[i][at : at + half].astype(jnp.bfloat16)

        def query_side():
            query_first = cols_dot(slopes_first, key_first)
            query_rest = cols_dot(slopes_rest, key_rest)
            query_grad = (
                jnp.concatenate([query_first[:lanes], query_first[lanes:] + query_rest], axis=0)
                * scale
            ).astype(jnp.bfloat16)
            for k in range(group):
                out = pl.ds((kv_head * group + k) * HD, HD)
                dq[lo, out] = query_grad[k * half : (k + 1) * half]
                dq[hi, out] = query_grad[lanes + k * half : lanes + (k + 1) * half]

        return query_side

    def stage_arrive(c):
        for d in range(1, n):
            to_part(d, c, False).wait_recv()
            to_far(d, c).start()
            if c + 2 < chunks:
                to_part(d, c + 2, True).start()
        if c == 0:
            loads[2].wait()
            loads[3].wait()
        for index in range(heads_in):
            first_logits(c * heads_in + index)

    def stage_compute(c):
        if c == 0:
            to_near().wait_recv()
        for d in range(1, n):
            to_far(d, c).wait_recv()
            to_part(d, c, True).wait_recv()
        query_sides = [one_head(c * heads_in + index) for index in range(heads_in)]
        to_prev(c).start()
        for d in range(1, n):
            to_late(d, c).start()
        for query_side in query_sides:
            query_side()
        dq_copy(c).start()

    def stage_front(c):
        to_prev(c).wait_recv()
        for d in range(1, n):
            for i in range(2):
                spot = (d - 1, i, pl.ds(0, half), span(c))
                total = part_out[spot].astype(jnp.float32)
                total = total + prev_in[d, i, :, span(c)].astype(jnp.float32)
                part_out[spot] = total.astype(jnp.bfloat16)
            to_front(d, c).start()

    def stage_finish(c):
        for d in range(1, n):
            to_late(d, c).wait_recv()
            to_front(d, c).wait_recv()
        for i in range(2):
            total = own_grad[i, :, span(c)]
            for d in range(1, n):
                total = total + part_in[d - 1, i, :, span(c)].astype(jnp.float32)
            front = total[:half] + prev_in[0, i, :, span(c)].astype(jnp.float32)
            result[i, pl.ds(0, half), span(c)] = front.astype(jnp.bfloat16)
            result[i, pl.ds(half, half), span(c)] = total[half:].astype(jnp.bfloat16)
            out_copy(i, c).start()

    for c in range(chunks):
        stage_arrive(c)
    for t in range(chunks + 2):
        if t < chunks:
            stage_compute(t)
        if t >= 2:
            stage_front(t - 2)
    for c in range(chunks):
        stage_finish(c)
    for c in range(chunks):
        if c == 0:
            to_near().wait_send()
        to_prev(c).wait_send()
        for d in range(1, n):
            to_part(d, c, False).wait_send()
            to_part(d, c, True).wait_send()
            to_far(d, c).wait_send()
            to_late(d, c).wait_send()
            to_front(d, c).wait_send()
        dq_copy(c).wait()
        out_copy(0, c).wait()
        out_copy(1, c).wait()


def hand_over(a, b, c, a_out, b_out, c_out, sem):
    rows = a.shape[0] // 4
    pairs = [(b, b_out), (c, c_out)]
    for i in range(4):
        pairs.append((a.at[pl.ds(i * rows, rows)], a_out.at[pl.ds(i * rows, rows)]))
    copies = [
        pltpu.make_async_copy(src, dst, sem.at[i]) for i, (src, dst) in enumerate(pairs)
    ]
    for copy in copies:
        copy.start()
    for copy in copies:
        copy.wait()


def solution(mesh):
    n, m = mesh.shape["head"], mesh.shape["blk"]

    def body(queries, keys, values, grad_out, order):
        rows, query_cols = queries.shape
        key_cols = keys.shape[1]
        half = rows // 2
        chunks = min(CHUNKS, key_cols // HD)
        lanes = half * (query_cols // key_cols)
        low, wide = jnp.bfloat16, jnp.float32
        dma = pltpu.SemaphoreType.DMA
        anywhere = pl.BlockSpec(memory_space=pl.ANY)
        grads = pl.pallas_call(
            functools.partial(kernel, n, m, order.shape[0], chunks),
            out_shape=(
                jax.ShapeDtypeStruct(queries.shape, low),
                jax.ShapeDtypeStruct(keys.shape, low),
                jax.ShapeDtypeStruct(values.shape, low),
            ),
            in_specs=[anywhere] * 5,
            out_specs=[anywhere] * 3,
            scratch_shapes=[
                pltpu.VMEM((rows, query_cols), low),
                pltpu.VMEM((rows, query_cols), low),
                pltpu.VMEM((rows, query_cols), low),
                pltpu.VMEM((2, rows, key_cols), low),
                pltpu.VMEM((n - 1, 2, rows, key_cols), low),
                pltpu.VMEM((n, 2, half, key_cols), low),
                pltpu.VMEM((2, rows, key_cols), wide),
                pltpu.VMEM((n, 2, half, key_cols), low),
                pltpu.VMEM((n, 2, half, key_cols), low),
                pltpu.VMEM((n - 1, 2, rows, key_cols), low),
                pltpu.VMEM((n - 1, 2, rows, key_cols), low),
                pltpu.VMEM((2, rows, key_cols), low),
                pltpu.VMEM((n * half, 2 * lanes), wide),
                pltpu.VMEM((2 * n * half, lanes), wide),
                pltpu.SMEM(order.shape, order.dtype),
                pltpu.VMEM((key_cols // HD, 2, n * half, 2 * lanes), wide),
                dma((5,)),
                dma((n - 1, chunks)), dma((n - 1, chunks)),
                dma((n - 1, chunks)), dma((n - 1, chunks)),
                dma((chunks,)), dma((chunks,)),
                dma((n - 1, chunks)), dma((n - 1, chunks)),
                dma((chunks,)), dma((chunks,)),
                dma((n - 1, chunks)), dma((n - 1, chunks)),
                dma((n - 1, chunks)), dma((n - 1, chunks)),
                dma((chunks,)), dma((2, chunks)),
            ],
            compiler_params=pltpu.CompilerParams(
                collective_id=0, has_side_effects=True, vmem_limit_bytes=40 * 2**20
            ),
        )(*(
            pltpu.with_memory_space_constraint(x, pltpu.HBM)
            for x in (order, queries, keys, values, grad_out)
        ))
        return pl.pallas_call(
            hand_over,
            out_shape=tuple(jax.ShapeDtypeStruct(x.shape, x.dtype) for x in grads),
            in_specs=[anywhere] * 3,
            out_specs=[anywhere] * 3,
            scratch_shapes=[dma((6,))],
            compiler_params=pltpu.CompilerParams(vmem_limit_bytes=2**20),
        )(*grads)

    shard = P(("head", "blk"), None)
    return jax.shard_map(
        body,
        mesh=mesh,
        in_specs=(shard, shard, shard, shard, P()),
        out_specs=(shard, shard, shard),
        check_vma=False,
    )
```
